512 devices in a mesh: tok: 16 (over z, core), hid: 32 (over y, x).
Axes of the slice: x: 4, y: 8, z: 8, core: 2. Of those that a mesh axis runs over, the one named last changes fastest.
Arguments:
- activations: bfloat16 [2048, 4096], P('tok'), may hold values from -12 to 12
- cotangent: bfloat16 [2048, 8192], P('tok', 'hid'), may hold values from -0.0078125 to 0.0078125
- left_gram: float32 [32, 1024, 1024], P('hid', 'tok'), may hold values from -0.28125 to 30, as said below
- right_gram: float32 [32, 1024, 1024], P('hid', 'tok'), may hold values from -0.28125 to 30, as said below
- left_root: float32 [32, 1024, 1024], P('hid', 'tok'), may hold values from -0.0115625 to 1.21, as said below
- right_root: float32 [32, 1024, 1024], P('hid', 'tok'), may hold values from -0.0115625 to 1.21, as said below
Outputs:
- left_next: float32 [32, 1024, 1024], P('hid', 'tok')
- right_next: float32 [32, 1024, 1024], P('hid', 'tok')
- left_refined: float32 [32, 1024, 1024], P('hid', 'tok')
- right_refined: float32 [32, 1024, 1024], P('hid', 'tok')
- update: float32 [4, 1024, 8192], P(None, 'tok', 'hid')
The draws below stay inside these ranges and needn't reach their ends.
Inputs may be any that keep to these rules, and one draw needn't show every extreme that they name: `left_gram`: every block is symmetric and positive definite. `right_gram`: every block is symmetric and positive definite. `left_root`: every block is symmetric. `right_root`: every block is symmetric.
All inputs are finite; a program needn't handle non-finite values.
Results may differ from the reference program's by a relative error of at most 0.019.
Values may be sent and summed in bfloat16 or wider, within the bound.
No kernel may reach another device: no remote copies, remote signals or barrier semaphores. Data moves between devices by JAX's collectives and lax.ppermute only.
A program may use at most 64 MiB of HBM per device.

```python
import jax
import jax.numpy as jnp
from jax import lax

DW = 4096
FF = 8192
BS = 1024
TOKENS = 2048
NBR = 4
NBC = 8
NB = 32
N_TOK = 16


def draw_activations(key, part):
    noise_key = jax.random.fold_in(key, 1)
    scale_key = jax.random.fold_in(key, 2)
    values = jnp.clip(jax.random.normal(noise_key, (TOKENS, DW), jnp.float32), -6.0, 6.0)
    rising = (jnp.arange(DW) % BS).astype(jnp.float32) / BS
    spread = jax.random.uniform(scale_key, (DW,), jnp.float32)
    scales = jnp.exp(jnp.log(2.0) * 0.5 * (spread + rising))
    return (values * scales[None, :]).astype(jnp.bfloat16)


def scales_from(unit):
    upper = 10.0
    return jnp.exp(unit * jnp.log(upper))


def coupling_from(raw):
    raw = 0.5 * (raw + jnp.swapaxes(raw, 1, 2))
    identity = jnp.eye(BS, dtype=jnp.float32)
    return raw * (1.0 - identity) * (0.3 / BS ** 0.5) + identity


def gram_from(unit, raw):
    scales = jnp.sqrt(scales_from(unit))
    return scales[:, :, None] * coupling_from(raw) * scales[:, None, :]


def root_from(unit, jitter, raw):
    factors = jitter * scales_from(unit) ** (-0.25)
    return factors[:, :, None] * coupling_from(raw) * factors[:, None, :]


def draw_left_gram(key, part):
    unit = jax.random.uniform(jax.random.fold_in(key, 11), (NB, BS), jnp.float32)
    raw = jax.random.uniform(jax.random.fold_in(key, 12), (NB, BS, BS), jnp.float32, -1.0, 1.0)
    return gram_from(unit, raw)


def draw_right_gram(key, part):
    unit = jax.random.uniform(jax.random.fold_in(key, 21), (NB, BS), jnp.float32)
    raw = jax.random.uniform(jax.random.fold_in(key, 22), (NB, BS, BS), jnp.float32, -1.0, 1.0)
    return gram_from(unit, raw)


def draw_left_root(key, part):
    unit = jax.random.uniform(jax.random.fold_in(key, 11), (NB, BS), jnp.float32)
    jitter = jax.random.uniform(jax.random.fold_in(key, 13), (NB, BS), jnp.float32, 0.9, 1.1)
    raw = jax.random.uniform(jax.random.fold_in(key, 14), (NB, BS, BS), jnp.float32, -1.0, 1.0)
    return root_from(unit, jitter, raw)


def draw_right_root(key, part):
    unit = jax.random.uniform(jax.random.fold_in(key, 21), (NB, BS), jnp.float32)
    jitter = jax.random.uniform(jax.random.fold_in(key, 23), (NB, BS), jnp.float32, 0.9, 1.1)
    raw = jax.random.uniform(jax.random.fold_in(key, 24), (NB, BS, BS), jnp.float32, -1.0, 1.0)
    return root_from(unit, jitter, raw)


def block_levels(own_key, shape, cuts, least, largest):
    def one(axis_at, blocks):
        heights = jax.random.uniform(jax.random.fold_in(jax.random.fold_in(own_key, 6), axis_at), (blocks,), jnp.float32, least / len(cuts), largest / len(cuts))
        return jnp.repeat(jnp.exp(heights), shape[axis_at] // blocks).reshape((-1,) + (1,) * (len(shape) - axis_at - 1))

    level = one(*cuts[0])
    for cut in cuts[1:]:
        level = level * one(*cut)
    return level


def bell_draw(own_key, shape, deviation, reach, cuts=(), kind=jnp.bfloat16):
    gain = block_levels(own_key, shape, cuts, -0.22, 0.18) if cuts else 1.0
    array = jax.random.normal(own_key, shape, jnp.float32) * deviation * gain
    return jnp.minimum(jnp.maximum(array, -reach), reach).astype(kind)


def setup_inputs(seed: int = 0) -> dict:
    key_list = jax.random.split(jax.random.key(seed), 7)
    activations = draw_activations(jax.random.fold_in(key_list[6], 71), 0)
    cotangent = bell_draw(key_list[1], (TOKENS, FF), (0.0221 / TOKENS ** 0.5), 0.0078125, ((0, 16), (1, 32)))
    left_gram = draw_left_gram(jax.random.fold_in(key_list[6], 71), 0)
    right_gram = draw_right_gram(jax.random.fold_in(key_list[6], 71), 0)
    left_root = draw_left_root(jax.random.fold_in(key_list[6], 71), 0)
    right_root = draw_right_root(jax.random.fold_in(key_list[6], 71), 0)
    return {"activations": activations, "cotangent": cotangent, "left_gram": left_gram, "right_gram": right_gram, "left_root": left_root, "right_root": right_root}


BETA = 0.95
EPS = 1e-06

def newton_root(gram_block, root_block, root_low):
    product = gram_block.astype(jnp.bfloat16)
    for repeat in range(4):
        product = jnp.dot(product, root_low, preferred_element_type=jnp.float32).astype(jnp.bfloat16)
    final = jnp.dot(product, root_low, preferred_element_type=jnp.float32)
    return (5.0 * root_block - final) / 4.0

def reference(activations, cotangent, left_gram, right_gram, left_root, right_root):
    shard_inputs = activations.reshape(N_TOK, TOKENS // N_TOK, DW)
    shard_cotangents = cotangent.reshape(N_TOK, TOKENS // N_TOK, FF)

    def accumulate(running, shards):
        partial_value = jnp.dot(shards[0].T, shards[1], preferred_element_type=jnp.float32)
        rounded = lax.optimization_barrier(partial_value.astype(jnp.bfloat16))
        return (running + rounded.astype(jnp.float32), None)
    gradient, unused = lax.scan(accumulate, jnp.zeros((DW, FF), jnp.float32), (shard_inputs, shard_cotangents))
    grad_low = gradient.astype(jnp.bfloat16)
    blocks = grad_low.reshape(NBR, BS, NBC, BS).transpose(2, 0, 1, 3).reshape(NB, BS, BS)

    def per_block(members):
        grad_block, left_old, right_old, left_current, right_current = members
        left_low = left_current.astype(jnp.bfloat16)
        right_low = right_current.astype(jnp.bfloat16)
        left_new = BETA * left_old + jnp.dot(grad_block, grad_block.T, preferred_element_type=jnp.float32)
        right_new = BETA * right_old + jnp.dot(grad_block.T, grad_block, preferred_element_type=jnp.float32)
        inner = jnp.dot(left_low, grad_block, preferred_element_type=jnp.float32).astype(jnp.bfloat16)
        precond = jnp.dot(inner, right_low, preferred_element_type=jnp.float32)
        scale = jnp.sqrt(jnp.sum(precond * precond) / (BS * BS) + EPS)
        return (left_new, right_new, newton_root(left_new, left_current, left_low), newton_root(right_new, right_current, right_low), precond / scale)
    results = lax.map(per_block, (blocks, left_gram, right_gram, left_root, right_root))
    update = results[4].reshape(NBC, NBR, BS, BS).transpose(1, 2, 0, 3).reshape(NBR, BS, FF)
    return (results[0], results[1], results[2], results[3], update)
```

```python
import functools

import jax
import jax.numpy as jnp
from jax import lax
from jax.experimental import pallas as pl
from jax.experimental.pallas import tpu as pltpu
from jax.sharding import Mesh
from jax.sharding import PartitionSpec as P

BETA = 0.95
EPS = 1e-06
F32 = jnp.float32
BF16 = jnp.bfloat16
NZ, NC, NY, NX = 8, 2, 8, 4
BS = 1024
HALF = BS // NC
ROWS = BS // (NZ * NC)
WIDTH = BS // NX
TOK = ("z", "core")
HID = ("y", "x")
SWAP = [(0, 1), (1, 0)]
VMEM = pl.BlockSpec(memory_space=pltpu.VMEM)
SMEM = pl.BlockSpec(memory_space=pltpu.SMEM)
PARAMS = pltpu.CompilerParams(vmem_limit_bytes=48 * 1024 * 1024)


def dot(a, b, dims=((1,), (0,))):
    return lax.dot_general(a, b, (dims, ((), ())), preferred_element_type=F32)


def call(body, outs, specs, scratch=(), flops=0, moved=0):
    return pl.pallas_call(
        body,
        out_shape=outs,
        in_specs=specs,
        out_specs=jax.tree.map(lambda _: VMEM, outs),
        scratch_shapes=list(scratch),
        compiler_params=PARAMS,
        cost_estimate=pl.CostEstimate(flops=flops, bytes_accessed=moved, transcendentals=0),
    )


def partial_kernel(where, act, cot, more_act, more_cot, out):
    core = where[1]
    for r in range(NX):
        own = act[:, pl.ds(pl.multiple_of(r * BS + core * HALF, 128), HALF)]
        total = dot(own, cot[...], ((0,), (0,)))
        total += dot(more_act[:, r * HALF : (r + 1) * HALF], more_cot[...], ((0,), (0,)))
        out[r] = total.astype(BF16).reshape(NZ, ROWS, WIDTH)


def sum_kernel(parts, out):
    for x in range(NX):
        total = parts[x, 0].astype(F32)
        for z in range(1, NZ):
            total += parts[x, z].astype(F32)
        low = total.astype(BF16)
        for z in range(NZ):
            out[z, :, x * WIDTH : (x + 1) * WIDTH] = low


def precond_kernel(where, mine, other, left_root, right_low, out, squares):
    core = where[1]
    low = left_root[...].astype(BF16)
    first, second = low[:, :HALF], low[:, HALF:]
    own = jnp.where(core == 0, first.astype(F32), second.astype(F32)).astype(BF16)
    far = jnp.where(core == 0, second.astype(F32), first.astype(F32)).astype(BF16)
    applied = dot(own, mine[...]) + dot(far, other[...])
    precond = dot(applied.astype(BF16), right_low[...])
    for x in range(NX):
        out[x] = precond[:, x * WIDTH : (x + 1) * WIDTH].astype(BF16)
    squares[...] = jnp.full(squares.shape, jnp.sum(precond * precond), F32)


def factor_kernel(
    where, mine, other, left_gram, right_gram, left_root, right_root, left_power, right_power,
    left_next, right_next, left_refined, right_refined, whole, columns,
):
    z, core = where[0], where[1]
    whole[pl.ds(pl.multiple_of(core * HALF, HALF), HALF)] = mine[...]
    whole[pl.ds(pl.multiple_of((1 - core) * HALF, HALF), HALF)] = other[...]
    rows = whole[pl.ds(pl.multiple_of((z * NC + core) * ROWS, ROWS), ROWS)]
    left = BETA * left_gram[...] + dot(rows, whole[...], ((1,), (1,)))
    left_next[...] = left
    slab = whole[:, pl.ds(pl.multiple_of(z * NC * ROWS, 128), NC * ROWS)]
    columns[...] = slab.astype(F32).T
    turned = columns[pl.ds(pl.multiple_of(core * ROWS, ROWS), ROWS)].astype(BF16)
    right = BETA * right_gram[...] + dot(turned, whole[...])
    right_next[...] = right
    left_refined[...] = (5.0 * left_root[...] - dot(left.astype(BF16), left_power[...])) / 4.0
    right_refined[...] = (5.0 * right_root[...] - dot(right.astype(BF16), right_power[...])) / 4.0


def update_kernel(arrived, squares, out):
    for x in range(NX):
        total = jnp.sum(squares[x * NZ * NC : (x + 1) * NZ * NC], axis=0)
        scale = 1.0 / jnp.sqrt(total / (BS * BS) + EPS)
        for part in range(WIDTH // 128):
            cols = slice(part * 128, (part + 1) * 128)
            out[x, :, cols] = arrived[x, :, cols].astype(F32) * scale


def on_device(activations, cotangent, left_gram, right_gram, left_root, right_root):
    left_gram, right_gram = left_gram[0], right_gram[0]
    left_root, right_root = left_root[0], right_root[0]
    z, core = lax.axis_index("z"), lax.axis_index("core")
    where = jnp.stack([z, core]).astype(jnp.int32)
    even = core == 0

    left_low, right_low = left_root.astype(BF16), right_root.astype(BF16)
    sent = jnp.where(even, right_low, left_low)
    kept = jnp.where(even, left_low, right_low)
    got = lax.ppermute(sent, "core", SWAP)
    shard = jnp.concatenate([jnp.where(even, kept, got), jnp.where(even, got, kept)], axis=0)
    root = lax.all_gather(shard, "z", axis=0, tiled=True)

    halves = [
        (activations[:, r * BS : r * BS + HALF], activations[:, r * BS + HALF : (r + 1) * BS])
        for r in range(NX)
    ]
    lent = jnp.concatenate([jnp.where(even, b, a) for a, b in halves], axis=1)
    more_act = lax.ppermute(lent, "core", SWAP)
    more_cot = lax.ppermute(cotangent, "core", SWAP)
    partial = call(
        partial_kernel, jax.ShapeDtypeStruct((NX, NZ, ROWS, WIDTH), BF16),
        [SMEM, VMEM, VMEM, VMEM, VMEM], flops=2 * 256 * 2048 * 256, moved=3_000_000,
    )(where, activations, cotangent, more_act, more_cot)
    parts = lax.all_to_all(
        partial.reshape(NX * NZ, ROWS, WIDTH), ("x", "z"), 0, 0, tiled=True
    ).reshape(NX, NZ, ROWS, WIDTH)
    copies = call(
        sum_kernel, jax.ShapeDtypeStruct((NZ, ROWS, BS), BF16), [VMEM], flops=1_000_000, moved=2_000_000
    )(parts)
    mine = lax.all_to_all(copies, "z", 0, 0, tiled=True).reshape(HALF, BS)
    other = lax.ppermute(mine, "core", SWAP)

    squared = dot(root, root).astype(BF16)
    fourth = dot(squared, squared).astype(BF16)
    fifth = dot(fourth, root).astype(BF16)
    far_root = lax.ppermute(root, "core", SWAP)
    far_fifth = lax.ppermute(fifth, "core", SWAP)
    right_whole = jnp.where(even, far_root, root)
    left_power = jnp.where(even, fifth, far_fifth)
    right_power = jnp.where(even, far_fifth, fifth)

    precond, squares = call(
        precond_kernel,
        (
            jax.ShapeDtypeStruct((NX, ROWS, WIDTH), BF16),
            jax.ShapeDtypeStruct((NX * NZ * NC, 1, 128), F32),
        ),
        [SMEM] + [VMEM] * 4, flops=4 * 64 * 1024 * 1024, moved=5_000_000,
    )(where, mine, other, left_root, right_whole)
    arrived = lax.all_to_all(precond, "x", 0, 0, tiled=True)
    sums = lax.all_to_all(squares, ("x", "z", "core"), 0, 0, tiled=True)
    shape = jax.ShapeDtypeStruct((ROWS, BS), F32)
    outs = call(
        factor_kernel, (shape,) * 4, [SMEM] + [VMEM] * 8,
        scratch=[pltpu.VMEM((BS, BS), BF16), pltpu.VMEM((NC * ROWS, BS), F32)],
        flops=8 * 64 * 1024 * 1024, moved=8_000_000,
    )(where, mine, other, left_gram, right_gram, left_root, right_root, left_power, right_power)
    update = call(
        update_kernel, jax.ShapeDtypeStruct((NX, ROWS, WIDTH), F32), [VMEM, VMEM],
        flops=100_000, moved=500_000,
    )(arrived, sums)
    return (*(o[None] for o in outs), update)


def solution(mesh):
    split = Mesh(mesh.devices.reshape(NZ, NC, NY, NX), (*TOK, *HID))
    factor = P(HID, TOK, None)
    return jax.shard_map(
        on_device,
        mesh=split,
        in_specs=(P(TOK, None), P(TOK, HID), factor, factor, factor, factor),
        out_specs=(factor, factor, factor, factor, P(None, TOK, HID)),
        check_vma=False,
    )
```

```python
import functools

import jax
import jax.numpy as jnp
from jax import lax
from jax.experimental import pallas as pl
from jax.experimental.pallas import tpu as pltpu
from jax.sharding import Mesh
from jax.sharding import PartitionSpec as P

BETA = 0.95
EPS = 1e-06
F32 = jnp.float32
BF16 = jnp.bfloat16
NZ, NC, NY, NX = 8, 2, 8, 4
BS = 1024
HALF = BS // NC
TOKENS = 128
ROWS = BS // (NZ * NC)
WIDTH = BS // NX
COT = NX * HALF
ROOT = COT + WIDTH
TILE = 256
TOK = ("z", "core")
HID = ("y", "x")
SWAP = [(0, 1), (1, 0)]
VMEM = pl.BlockSpec(memory_space=pltpu.VMEM)
SMEM = pl.BlockSpec(memory_space=pltpu.SMEM)
PARAMS = pltpu.CompilerParams(vmem_limit_bytes=48 * 1024 * 1024)


def dot(a, b, dims=((1,), (0,))):
    return lax.dot_general(a, b, (dims, ((), ())), preferred_element_type=F32)


def call(body, outs, specs, scratch=(), flops=0, moved=0):
    return pl.pallas_call(
        body,
        out_shape=outs,
        in_specs=specs,
        out_specs=jax.tree.map(lambda _: VMEM, outs),
        scratch_shapes=list(scratch),
        compiler_params=PARAMS,
        cost_estimate=pl.CostEstimate(flops=flops, bytes_accessed=moved, transcendentals=0),
    )


def pack_kernel(where, act, cot, left_root, right_root, out):
    core = where[1]
    for r in range(NX):
        far = act[:, pl.ds(pl.multiple_of(r * BS + (1 - core) * HALF, 128), HALF)]
        out[:, r * HALF : (r + 1) * HALF] = far
    out[:, COT : COT + WIDTH] = cot[...]
    lent = jnp.where(core == 0, right_root[...], left_root[...]).astype(BF16)
    out[:ROWS, ROOT:] = lent[:, :HALF]
    out[ROWS:, ROOT:] = lent[:, HALF:]


def partial_kernel(where, act, cot, left_root, right_root, more, out, shard):
    core = where[1]
    kept = jnp.where(core == 0, left_root[...], right_root[...]).astype(BF16)
    shard[pl.ds(pl.multiple_of(core * ROWS, ROWS), ROWS)] = kept
    far = pl.ds(pl.multiple_of((1 - core) * ROWS, ROWS), ROWS)
    shard[far, :HALF] = more[:ROWS, ROOT:]
    shard[far, HALF:] = more[ROWS:, ROOT:]
    more_cot = more[:, COT : COT + WIDTH]
    for r in range(NX):
        own = act[:, pl.ds(pl.multiple_of(r * BS + core * HALF, 128), HALF)]
        total = dot(own, cot[...], ((0,), (0,)))
        total += dot(more[:, r * HALF : (r + 1) * HALF], more_cot, ((0,), (0,)))
        out[r] = total.astype(BF16).reshape(NZ, ROWS, WIDTH)


def sum_kernel(parts, out):
    for x in range(NX):
        total = parts[x, 0].astype(F32)
        for z in range(1, NZ):
            total += parts[x, z].astype(F32)
        low = total.astype(BF16)
        for z in range(NZ):
            out[z, :, x * WIDTH : (x + 1) * WIDTH] = low


def power_kernel(root, fifth, squared, fourth):
    def times(a, b, out):
        def tile(i, carry):
            rows = pl.ds(pl.multiple_of(i * TILE, TILE), TILE)
            out[rows] = dot(a[rows], b[...]).astype(BF16)
            return carry

        lax.fori_loop(0, BS // TILE, tile, 0)

    times(root, root, squared)
    times(squared, squared, fourth)
    times(fourth, root, fifth)


def precond_kernel(where, mine, other, root, far_root, out, kept):
    z, core = where[0], where[1]
    place = (z * NC + core) * ROWS

    def run(left, right, upper, lower):
        def tile(i, total):
            rows = pl.ds(pl.multiple_of(i * TILE, TILE), TILE)
            applied = dot(left[rows, :HALF], upper[...]) + dot(left[rows, HALF:], lower[...])
            precond = dot(applied.astype(BF16), right[...])

            @pl.when(i == place // TILE)
            def _():
                kept[...] = precond

            return total + jnp.sum(precond * precond, axis=0, keepdims=True)

        total = lax.fori_loop(0, BS // TILE, tile, jnp.zeros((1, BS), F32))
        scale = 1.0 / jnp.sqrt(jnp.sum(total) / (BS * BS) + EPS)
        scaled = kept[pl.ds(pl.multiple_of(place % TILE, ROWS), ROWS)] * scale
        for x in range(NX):
            out[x] = scaled[:, x * WIDTH : (x + 1) * WIDTH].astype(BF16)

    @pl.when(core == 0)
    def _():
        run(root, far_root, mine, other)

    @pl.when(core == 1)
    def _():
        run(far_root, root, other, mine)


def factor_kernel(
    where, mine, other, left_gram, right_gram, left_root, right_root, fifth, far_fifth,
    left_next, right_next, left_refined, right_refined, whole, columns,
):
    z, core = where[0], where[1]
    even = core == 0
    whole[pl.ds(pl.multiple_of(core * HALF, HALF), HALF)] = mine[...]
    whole[pl.ds(pl.multiple_of((1 - core) * HALF, HALF), HALF)] = other[...]
    rows = whole[pl.ds(pl.multiple_of((z * NC + core) * ROWS, ROWS), ROWS)]
    left = BETA * left_gram[...] + dot(rows, whole[...], ((1,), (1,)))
    left_next[...] = left
    slab = whole[:, pl.ds(pl.multiple_of(z * NC * ROWS, 128), NC * ROWS)]
    columns[...] = slab.astype(F32).T
    turned = columns[pl.ds(pl.multiple_of(core * ROWS, ROWS), ROWS)].astype(BF16)
    right = BETA * right_gram[...] + dot(turned, whole[...])
    right_next[...] = right
    own = dot(jnp.where(even, left, right).astype(BF16), fifth[...])
    far = dot(jnp.where(even, right, left).astype(BF16), far_fifth[...])
    left_refined[...] = (5.0 * left_root[...] - jnp.where(even, own, far)) / 4.0
    right_refined[...] = (5.0 * right_root[...] - jnp.where(even, far, own)) / 4.0


def on_device(activations, cotangent, left_gram, right_gram, left_root, right_root):
    left_gram, right_gram = left_gram[0], right_gram[0]
    left_root, right_root = left_root[0], right_root[0]
    z, core = lax.axis_index("z"), lax.axis_index("core")
    where = jnp.stack([z, core]).astype(jnp.int32)
    even = core == 0

    packed = call(
        pack_kernel, jax.ShapeDtypeStruct((TOKENS, ROOT + HALF), BF16), [SMEM] + [VMEM] * 4,
        flops=100_000, moved=1_500_000,
    )(where, activations, cotangent, left_root, right_root)
    more = lax.ppermute(packed, "core", SWAP)
    partial, shard = call(
        partial_kernel,
        (
            jax.ShapeDtypeStruct((NX, NZ, ROWS, WIDTH), BF16),
            jax.ShapeDtypeStruct((NC * ROWS, BS), BF16),
        ),
        [SMEM] + [VMEM] * 5, flops=2 * 256 * 2048 * 256, moved=3_000_000,
    )(where, activations, cotangent, left_root, right_root, more)
    root = lax.all_gather(shard, "z", axis=0, tiled=True)
    parts = lax.all_to_all(
        partial.reshape(NX * NZ, ROWS, WIDTH), ("x", "z"), 0, 0, tiled=True
    ).reshape(NX, NZ, ROWS, WIDTH)
    copies = call(
        sum_kernel, jax.ShapeDtypeStruct((NZ, ROWS, BS), BF16), [VMEM], flops=1_000_000, moved=2_000_000
    )(parts)
    mine = lax.all_to_all(copies, "z", 0, 0, tiled=True).reshape(HALF, BS)
    other = lax.ppermute(mine, "core", SWAP)

    far_root = lax.ppermute(root, "core", SWAP)
    square = jax.ShapeDtypeStruct((BS, BS), BF16)
    fifth = call(
        power_kernel, square, [VMEM], scratch=[pltpu.VMEM((BS, BS), BF16)] * 2,
        flops=6 * BS**3, moved=4_000_000,
    )(root)
    far_fifth = lax.ppermute(fifth, "core", SWAP)

    precond = call(
        precond_kernel, jax.ShapeDtypeStruct((NX, ROWS, WIDTH), BF16), [SMEM] + [VMEM] * 4,
        scratch=[pltpu.VMEM((TILE, BS), F32)], flops=4 * BS**3, moved=6_000_000,
    )(where, mine, other, root, far_root)
    arrived = lax.all_to_all(precond, "x", 0, 0, tiled=True)
    shape = jax.ShapeDtypeStruct((ROWS, BS), F32)
    outs = call(
        factor_kernel, (shape,) * 4, [SMEM] + [VMEM] * 8,
        scratch=[pltpu.VMEM((BS, BS), BF16), pltpu.VMEM((NC * ROWS, BS), F32)],
        flops=8 * 64 * 1024 * 1024, moved=8_000_000,
    )(where, mine, other, left_gram, right_gram, left_root, right_root, fifth, far_fifth)
    return (*(o[None] for o in outs), arrived.astype(F32))


def solution(mesh):
    split = Mesh(mesh.devices.reshape(NZ, NC, NY, NX), (*TOK, *HID))
    factor = P(HID, TOK, None)
    return jax.shard_map(
        on_device,
        mesh=split,
        in_specs=(P(TOK, None), P(TOK, HID), factor, factor, factor, factor),
        out_specs=(factor, factor, factor, factor, P(None, TOK, HID)),
        check_vma=False,
    )
```

```python
import jax
import jax.numpy as jnp
from jax import lax
from jax.experimental import pallas as pl
from jax.experimental.pallas import tpu as pltpu
from jax.sharding import Mesh
from jax.sharding import PartitionSpec as P

BETA = 0.95
EPS = 1e-06
F32 = jnp.float32
BF16 = jnp.bfloat16
NZ, NC, NY, NX = 8, 2, 8, 4
BS = 1024
HALF = BS // NC
TOKENS = 128
ROWS = BS // (NZ * NC)
WIDTH = BS // NX
COT = NX * HALF
ROOT = COT + WIDTH
TILE = 512
SIDE = NC * ROWS
OFF = 3
STRIP = OFF * 2 * SIDE + SIDE
SLABS = NX * ROWS
CHUNK = SLABS + ROWS + ROWS // 2
TOK = ("z", "core")
HID = ("y", "x")
SWAP = [(0, 1), (1, 0)]
VMEM = pl.BlockSpec(memory_space=pltpu.VMEM)
SMEM = pl.BlockSpec(memory_space=pltpu.SMEM)
HBM = pl.BlockSpec(memory_space=pltpu.HBM)
PARAMS = pltpu.CompilerParams(vmem_limit_bytes=48 * 1024 * 1024)


def dot(a, b, dims=((1,), (0,))):
    return lax.dot_general(a, b, (dims, ((), ())), preferred_element_type=F32)


def call(body, outs, specs, scratch=(), flops=0, moved=0):
    return pl.pallas_call(
        body,
        out_shape=outs,
        in_specs=specs,
        out_specs=jax.tree.map(lambda _: VMEM, outs),
        scratch_shapes=list(scratch),
        compiler_params=PARAMS,
        cost_estimate=pl.CostEstimate(flops=flops, bytes_accessed=moved, transcendentals=0),
    )


def at(start, size, unit):
    return pl.ds(pl.multiple_of(start, unit), size)


def pack_kernel(where, act, cot, left_root, right_root, own, far, roots, sems):
    core = where[1]
    copies = []
    for k, (out, side) in enumerate(((far, 1 - core), (own, core))):
        for r in range(NX):
            source = act.at[:, at(r * BS + side * HALF, HALF, 128)]
            target = out.at[:, pl.ds(r * HALF, HALF)]
            copies.append(pltpu.make_async_copy(source, target, sems.at[k, r]))
        copies.append(pltpu.make_async_copy(cot, out.at[:, pl.ds(COT, WIDTH)], sems.at[k, NX]))
    copies.append(pltpu.make_async_copy(left_root, roots.at[0], sems.at[0, NX + 1]))
    copies.append(pltpu.make_async_copy(right_root, roots.at[1], sems.at[1, NX + 1]))
    for copy in copies:
        copy.start()
    for copy in copies:
        copy.wait()
    for out, side in ((far, 1 - core), (own, core)):
        low = roots[side].astype(BF16)
        out[:ROWS, ROOT:] = low[:, :HALF]
        out[ROWS:, ROOT:] = low[:, HALF:]


def partial_kernel(where, own, more, out, strip, shard):
    z, core = where[0], where[1]
    for r in range(NX):
        cols = slice(r * HALF, (r + 1) * HALF)
        total = dot(own[:, cols], own[:, COT : COT + WIDTH], ((0,), (0,)))
        total += dot(more[:, cols], more[:, COT : COT + WIDTH], ((0,), (0,)))
        low = total.astype(BF16)
        for to in range(NZ):
            out[to, r * ROWS : (r + 1) * ROWS] = low[to * ROWS : (to + 1) * ROWS]
    for given, side in ((own, core), (more, 1 - core)):
        rows = at(side * ROWS, ROWS, ROWS)
        shard[rows, :HALF] = given[:ROWS, ROOT:]
        shard[rows, HALF:] = given[ROWS:, ROOT:]

    def block(k):
        return shard[:, at(lax.rem(z + k, NZ) * SIDE, SIDE, SIDE)]

    for k in range(1, OFF + 1):
        piece, first = block(k), (k - 1) * 2 * SIDE
        strip[:, first : first + SIDE] = piece[:ROWS]
        strip[:, first + SIDE : first + 2 * SIDE] = piece[ROWS:]
    middle, across = block(0), block(OFF + 1)
    strip[:, OFF * 2 * SIDE :] = across[:ROWS]
    for to in range(NZ):
        out[to, SLABS : SLABS + ROWS, :SIDE] = middle[:ROWS]
        out[to, SLABS : SLABS + ROWS, SIDE:] = middle[ROWS:]
        out[to, SLABS + ROWS :, :SIDE] = across[ROWS : ROWS + ROWS // 2]
        out[to, SLABS + ROWS :, SIDE:] = across[ROWS + ROWS // 2 :]


def sum_kernel(parts, out):
    for x in range(NX):
        rows = slice(x * ROWS, (x + 1) * ROWS)
        total = parts[0, rows].astype(F32)
        for z in range(1, NZ):
            total += parts[z, rows].astype(F32)
        low = total.astype(BF16)
        for z in range(NZ):
            out[x, z] = low


def root_kernel(strips, parts, root):
    for z in range(NZ):
        top, low = slice(z * SIDE, z * SIDE + ROWS), slice(z * SIDE + ROWS, (z + 1) * SIDE)
        own = slice(z * SIDE, (z + 1) * SIDE)
        root[top, own] = parts[z, SLABS : SLABS + ROWS, :SIDE]
        root[low, own] = parts[z, SLABS : SLABS + ROWS, SIDE:]
        for k in range(1, OFF + 1):
            j, first = (z + k) % NZ, (k - 1) * 2 * SIDE
            piece = jnp.concatenate(
                [strips[z, :, first : first + SIDE], strips[z, :, first + SIDE : first + 2 * SIDE]],
                axis=0,
            )
            there = slice(j * SIDE, (j + 1) * SIDE)
            root[own, there] = piece
            root[there, own] = piece.T
        j = (z + OFF + 1) % NZ
        there = slice(j * SIDE, (j + 1) * SIDE)
        half = z * SIDE + ROWS + ROWS // 2
        root[top, there] = strips[z, :, OFF * 2 * SIDE :]
        root[z * SIDE + ROWS : half, there] = parts[z, SLABS + ROWS :, :SIDE]
        root[half : (z + 1) * SIDE, there] = parts[z, SLABS + ROWS :, SIDE:]


def precond_kernel(where, mine, other, root, far_root, out, kept):
    z, core = where[0], where[1]
    place = (z * NC + core) * ROWS

    def run(left, right, upper, lower):
        def tile(i, total):
            rows = at(i * TILE, TILE, TILE)
            first, second = left[rows, :HALF], left[rows, HALF:]
            applied = jnp.concatenate(
                [(dot(first, upper[x]) + dot(second, lower[x])).astype(BF16) for x in range(NX)],
                axis=1,
            )
            precond = dot(applied, right[...])

            @pl.when(i == place // TILE)
            def _():
                kept[...] = precond

            return total + jnp.sum(precond * precond, axis=0, keepdims=True)

        total = lax.fori_loop(0, BS // TILE, tile, jnp.zeros((1, BS), F32))
        scale = 1.0 / jnp.sqrt(jnp.sum(total) / (BS * BS) + EPS)
        scaled = kept[at(place % TILE, ROWS, ROWS)] * scale
        for x in range(NX):
            out[x] = scaled[:, x * WIDTH : (x + 1) * WIDTH].astype(BF16)

    @pl.when(core == 0)
    def _():
        run(root, far_root, mine, other)

    @pl.when(core == 1)
    def _():
        run(far_root, root, other, mine)


def power_kernel(root, fifth, squared, fourth):
    def times(a, b, out):
        def tile(i, carry):
            rows = at(i * TILE, TILE, TILE)
            out[rows] = dot(a[rows], b[...]).astype(BF16)
            return carry

        lax.fori_loop(0, BS // TILE, tile, 0)

    times(root, root, squared)
    times(squared, squared, fourth)
    times(fourth, root, fifth)


def factor_kernel(
    where, mine, other, left_gram, right_gram, left_root, right_root, fifth, far_fifth,
    left_next, right_next, left_refined, right_refined, whole, columns, old, sems,
):
    z, core = where[0], where[1]
    even = core == 0
    copies = [
        pltpu.make_async_copy(source, old.at[k], sems.at[k])
        for k, source in enumerate((left_gram, right_gram, left_root, right_root))
    ]
    for copy in copies:
        copy.start()
    for x in range(NX):
        whole[at(core * HALF, HALF, HALF), x * WIDTH : (x + 1) * WIDTH] = mine[x]
        whole[at((1 - core) * HALF, HALF, HALF), x * WIDTH : (x + 1) * WIDTH] = other[x]
    slab = whole[:, at(z * SIDE, SIDE, SIDE)]
    columns[...] = slab.astype(F32).T
    rows = whole[at((z * NC + core) * ROWS, ROWS, ROWS)]
    left = dot(rows, whole[...], ((1,), (1,)))
    turned = columns[at(core * ROWS, ROWS, ROWS)].astype(BF16)
    right = dot(turned, whole[...])
    for copy in copies:
        copy.wait()
    left = BETA * old[0] + left
    left_next[...] = left
    right = BETA * old[1] + right
    right_next[...] = right
    own = dot(jnp.where(even, left, right).astype(BF16), fifth[...])
    far = dot(jnp.where(even, right, left).astype(BF16), far_fifth[...])
    left_refined[...] = (5.0 * old[2] - jnp.where(even, own, far)) / 4.0
    right_refined[...] = (5.0 * old[3] - jnp.where(even, far, own)) / 4.0


def on_device(activations, cotangent, left_gram, right_gram, left_root, right_root):
    left_gram, right_gram = left_gram[0], right_gram[0]
    left_root, right_root = left_root[0], right_root[0]
    where = jnp.stack([lax.axis_index("z"), lax.axis_index("core")]).astype(jnp.int32)

    half = jax.ShapeDtypeStruct((TOKENS, ROOT + HALF), BF16)
    own, far = call(
        pack_kernel, (half, half), [SMEM] + [HBM] * 4,
        scratch=[pltpu.VMEM((2, ROWS, BS), F32), pltpu.SemaphoreType.DMA((2, NX + 2))],
        flops=100_000, moved=1_500_000,
    )(where, activations, cotangent, left_root, right_root)
    more = lax.ppermute(far, "core", SWAP)
    partial, strip = call(
        partial_kernel,
        (
            jax.ShapeDtypeStruct((NZ, CHUNK, WIDTH), BF16),
            jax.ShapeDtypeStruct((ROWS, STRIP), BF16),
        ),
        [SMEM, VMEM, VMEM], scratch=[pltpu.VMEM((SIDE, BS), BF16)],
        flops=2 * 256 * 2048 * 256, moved=3_000_000,
    )(where, own, more)
    parts = lax.all_to_all(partial, "z", 0, 0, tiled=True)
    strips = lax.all_gather(strip, "z", axis=0)
    parts, strips = lax.optimization_barrier((parts, strips))
    copies = call(
        sum_kernel, jax.ShapeDtypeStruct((NX, NZ, ROWS, WIDTH), BF16), [VMEM],
        flops=1_000_000, moved=2_000_000,
    )(parts)
    root = call(
        root_kernel, jax.ShapeDtypeStruct((BS, BS), BF16), [VMEM, VMEM], flops=1_000_000, moved=4_000_000
    )(strips, parts)
    far_root = lax.ppermute(root, "core", SWAP)
    fifth = call(
        power_kernel, jax.ShapeDtypeStruct((BS, BS), BF16), [VMEM],
        scratch=[pltpu.VMEM((BS, BS), BF16)] * 2, flops=6 * BS**3, moved=4_000_000,
    )(root)
    far_fifth = lax.ppermute(fifth, "core", SWAP)
    mine = lax.all_to_all(
        copies.reshape(NX * NZ, ROWS, WIDTH), ("x", "z"), 0, 0, tiled=True
    ).reshape(NX, HALF, WIDTH)
    other = lax.ppermute(mine, "core", SWAP)

    precond = call(
        precond_kernel, jax.ShapeDtypeStruct((NX, ROWS, WIDTH), BF16), [SMEM] + [VMEM] * 4,
        scratch=[pltpu.VMEM((TILE, BS), F32)], flops=4 * BS**3, moved=6_000_000,
    )(where, mine, other, root, far_root)
    arrived = lax.all_to_all(precond, "x", 0, 0, tiled=True)
    shape = jax.ShapeDtypeStruct((ROWS, BS), F32)
    outs = call(
        factor_kernel, (shape,) * 4, [SMEM, VMEM, VMEM] + [HBM] * 4 + [VMEM] * 2,
        scratch=[
            pltpu.VMEM((BS, BS), BF16),
            pltpu.VMEM((SIDE, BS), F32),
            pltpu.VMEM((4, ROWS, BS), F32),
            pltpu.SemaphoreType.DMA((4,)),
        ],
        flops=8 * 64 * 1024 * 1024, moved=8_000_000,
    )(where, mine, other, left_gram, right_gram, left_root, right_root, fifth, far_fifth)
    return (*(o[None] for o in outs), arrived.astype(F32))


def solution(mesh):
    split = Mesh(mesh.devices.reshape(NZ, NC, NY, NX), (*TOK, *HID))
    factor = P(HID, TOK, None)
    return jax.shard_map(
        on_device,
        mesh=split,
        in_specs=(P(TOK, None), P(TOK, HID), factor, factor, factor, factor),
        out_specs=(factor, factor, factor, factor, P(None, TOK, HID)),
        check_vma=False,
    )
```

```python
import jax
import jax.numpy as jnp
from jax import lax
from jax.experimental import pallas as pl
from jax.experimental.pallas import tpu as pltpu
from jax.sharding import Mesh
from jax.sharding import PartitionSpec as P

BETA = 0.95
EPS = 1e-06
F32 = jnp.float32
BF16 = jnp.bfloat16
NZ, NC, NY, NX = 8, 2, 8, 4
BS = 1024
HALF = BS // NC
TOKENS = 128
ROWS = BS // (NZ * NC)
WIDTH = BS // NX
COT = NX * HALF
ROOT = COT + WIDTH
TILE = 512
SIDE = NC * ROWS
OFF = 3
SLABS = NX * ROWS
CHUNK = SLABS + (OFF + 1) * ROWS + ROWS
TOK = ("z", "core")
HID = ("y", "x")
SWAP = [(0, 1), (1, 0)]
VMEM = pl.BlockSpec(memory_space=pltpu.VMEM)
ANY = pl.BlockSpec(memory_space=pl.ANY)
HBM = pl.BlockSpec(memory_space=pltpu.HBM)
PARAMS = pltpu.CompilerParams(vmem_limit_bytes=28 * 1024 * 1024)


def dot(a, b, dims=((1,), (0,))):
    return lax.dot_general(a, b, (dims, ((), ())), preferred_element_type=F32)


def call(body, outs, specs, scratch=(), flops=0, moved=0):
    return pl.pallas_call(
        body,
        out_shape=outs,
        in_specs=specs,
        out_specs=jax.tree.map(lambda _: VMEM, outs),
        scratch_shapes=list(scratch),
        compiler_params=PARAMS,
        cost_estimate=pl.CostEstimate(flops=flops, bytes_accessed=moved, transcendentals=0),
    )


def in_hbm(value):
    return pltpu.with_memory_space_constraint(value, pltpu.HBM)


def at(start, size, unit):
    return pl.ds(pl.multiple_of(start, unit), size)


def pack_kernel(act, cot, left_root, right_root, own, far, roots, sems):
    core = lax.axis_index("core")
    copies = []
    for k, (out, side) in enumerate(((far, 1 - core), (own, core))):
        for r in range(NX):
            source = act.at[:, at(r * BS + side * HALF, HALF, 128)]
            target = out.at[:, pl.ds(r * HALF, HALF)]
            copies.append(pltpu.make_async_copy(source, target, sems.at[k, r]))
        copies.append(pltpu.make_async_copy(cot, out.at[:, pl.ds(COT, WIDTH)], sems.at[k, NX]))
    copies.append(pltpu.make_async_copy(left_root, roots.at[0], sems.at[0, NX + 1]))
    copies.append(pltpu.make_async_copy(right_root, roots.at[1], sems.at[1, NX + 1]))
    for copy in copies:
        copy.start()
    for copy in copies:
        copy.wait()
    for out, side in ((far, 1 - core), (own, core)):
        low = roots[side].astype(BF16)
        out[:ROWS, ROOT:] = low[:, :HALF]
        out[ROWS:, ROOT:] = low[:, HALF:]


def partial_kernel(own, more, out, shard):
    z, core = lax.axis_index("z"), lax.axis_index("core")
    for r in range(NX):
        cols = slice(r * HALF, (r + 1) * HALF)
        total = dot(own[:, cols], own[:, COT : COT + WIDTH], ((0,), (0,)))
        total += dot(more[:, cols], more[:, COT : COT + WIDTH], ((0,), (0,)))
        low = total.astype(BF16)
        for to in range(NZ):
            out[to, r * ROWS : (r + 1) * ROWS] = low[to * ROWS : (to + 1) * ROWS]
    for given, side in ((own, core), (more, 1 - core)):
        rows = at(side * ROWS, ROWS, ROWS)
        shard[rows, :HALF] = given[:ROWS, ROOT:]
        shard[rows, HALF:] = given[ROWS:, ROOT:]

    def block(k):
        return shard[:, at(lax.rem(z + k, NZ) * SIDE, SIDE, SIDE)]

    for k in range(OFF + 2):
        piece, first = block(k), SLABS + k * ROWS
        for to in range(NZ):
            out[to, first : first + ROWS, :SIDE] = piece[:ROWS]
            out[to, first : first + ROWS, SIDE:] = piece[ROWS:]


def sum_kernel(parts, out):
    for x in range(NX):
        rows = slice(x * ROWS, (x + 1) * ROWS)
        total = parts[0, rows].astype(F32)
        for z in range(1, NZ):
            total += parts[z, rows].astype(F32)
        low = total.astype(BF16)
        for z in range(NZ):
            out[x, z] = low


def root_kernel(parts, root):
    for z in range(NZ):
        own = slice(z * SIDE, (z + 1) * SIDE)
        for k in range(OFF + 2):
            j, first = (z + k) % NZ, SLABS + k * ROWS
            there = slice(j * SIDE, (j + 1) * SIDE)
            piece = jnp.concatenate(
                [parts[z, first : first + ROWS, :SIDE], parts[z, first : first + ROWS, SIDE:]], axis=0
            )
            root[own, there] = piece
            if 0 < k <= OFF:
                root[there, own] = piece.T


def precond_kernel(mine, other, root, far_root, out, kept):
    z, core = lax.axis_index("z"), lax.axis_index("core")
    place = (z * NC + core) * ROWS

    def run(left, right, upper, lower):
        def tile(i, total):
            rows = at(i * TILE, TILE, TILE)
            first, second = left[rows, :HALF], left[rows, HALF:]
            applied = jnp.concatenate(
                [(dot(first, upper[x]) + dot(second, lower[x])).astype(BF16) for x in range(NX)],
                axis=1,
            )
            precond = dot(applied, right[...])

            @pl.when(i == place // TILE)
            def _():
                kept[...] = precond

            return total + jnp.sum(precond * precond, axis=0, keepdims=True)

        total = lax.fori_loop(0, BS // TILE, tile, jnp.zeros((1, BS), F32))
        scale = 1.0 / jnp.sqrt(jnp.sum(total) / (BS * BS) + EPS)
        scaled = kept[at(place % TILE, ROWS, ROWS)] * scale
        for x in range(NX):
            out[x] = scaled[:, x * WIDTH : (x + 1) * WIDTH].astype(BF16)

    @pl.when(core == 0)
    def _():
        run(root, far_root, mine, other)

    @pl.when(core == 1)
    def _():
        run(far_root, root, other, mine)


def power_kernel(root, fifth, squared, fourth):
    def times(a, b, out):
        def tile(i, carry):
            rows = at(i * TILE, TILE, TILE)
            out[rows] = dot(a[rows], b[...]).astype(BF16)
            return carry

        lax.fori_loop(0, BS // TILE, tile, 0)

    times(root, root, squared)
    times(squared, squared, fourth)
    times(fourth, root, fifth)


def factor_kernel(
    mine, other, left_gram, right_gram, left_root, right_root, fifth, far_fifth,
    left_next, right_next, left_refined, right_refined, whole, columns, old, powers, sems,
):
    z, core = lax.axis_index("z"), lax.axis_index("core")
    even = core == 0
    pieces = []
    for k, (half, side) in enumerate(((mine, core), (other, 1 - core))):
        for x in range(NX):
            target = whole.at[at(side * HALF, HALF, HALF), pl.ds(x * WIDTH, WIDTH)]
            pieces.append(pltpu.make_async_copy(half.at[x], target, sems.at[k, x]))
    olds = [
        pltpu.make_async_copy(source, old.at[k], sems.at[2, k])
        for k, source in enumerate((left_gram, right_gram, left_root, right_root))
    ]
    both = [
        pltpu.make_async_copy(source, powers.at[k], sems.at[3, k])
        for k, source in enumerate((fifth, far_fifth))
    ]
    for copy in pieces + olds + both:
        copy.start()
    for copy in pieces:
        copy.wait()
    slab = whole[:, at(z * SIDE, SIDE, SIDE)]
    columns[...] = slab.astype(F32).T
    rows = whole[at((z * NC + core) * ROWS, ROWS, ROWS)]
    left = dot(rows, whole[...], ((1,), (1,)))
    turned = columns[at(core * ROWS, ROWS, ROWS)].astype(BF16)
    right = dot(turned, whole[...])
    for copy in olds + both:
        copy.wait()
    left = BETA * old[0] + left
    left_next[...] = left
    right = BETA * old[1] + right
    right_next[...] = right
    own = dot(jnp.where(even, left, right).astype(BF16), powers[0])
    far = dot(jnp.where(even, right, left).astype(BF16), powers[1])
    left_refined[...] = (5.0 * old[2] - jnp.where(even, own, far)) / 4.0
    right_refined[...] = (5.0 * old[3] - jnp.where(even, far, own)) / 4.0


def on_device(activations, cotangent, left_gram, right_gram, left_root, right_root):
    left_gram, right_gram = left_gram[0], right_gram[0]
    left_root, right_root = left_root[0], right_root[0]

    half = jax.ShapeDtypeStruct((TOKENS, ROOT + HALF), BF16)
    own, far = call(
        pack_kernel, (half, half), [HBM] * 4,
        scratch=[pltpu.VMEM((2, ROWS, BS), F32), pltpu.SemaphoreType.DMA((2, NX + 2))],
        flops=100_000, moved=1_500_000,
    )(*map(in_hbm, (activations, cotangent, left_root, right_root)))
    more = lax.ppermute(far, "core", SWAP)
    partial = call(
        partial_kernel, jax.ShapeDtypeStruct((NZ, CHUNK, WIDTH), BF16),
        [VMEM, VMEM], scratch=[pltpu.VMEM((SIDE, BS), BF16)],
        flops=2 * 256 * 2048 * 256, moved=3_000_000,
    )(own, more)
    parts = lax.all_to_all(partial, "z", 0, 0, tiled=True)
    copies = call(
        sum_kernel, jax.ShapeDtypeStruct((NX, NZ, ROWS, WIDTH), BF16), [VMEM],
        flops=1_000_000, moved=2_000_000,
    )(parts)
    root = call(
        root_kernel, jax.ShapeDtypeStruct((BS, BS), BF16), [VMEM], flops=1_000_000, moved=4_000_000
    )(parts)
    far_root = lax.ppermute(root, "core", SWAP)
    fifth = call(
        power_kernel, jax.ShapeDtypeStruct((BS, BS), BF16), [VMEM],
        scratch=[pltpu.VMEM((BS, BS), BF16)] * 2, flops=6 * BS**3, moved=4_000_000,
    )(root)
    far_fifth = lax.ppermute(fifth, "core", SWAP)
    mine = lax.all_to_all(
        copies.reshape(NX * NZ, ROWS, WIDTH), ("x", "z"), 0, 0, tiled=True
    ).reshape(NX, HALF, WIDTH)
    other = lax.ppermute(mine, "core", SWAP)

    precond = call(
        precond_kernel, jax.ShapeDtypeStruct((NX, ROWS, WIDTH), BF16), [VMEM] * 4,
        scratch=[pltpu.VMEM((TILE, BS), F32)], flops=4 * BS**3, moved=6_000_000,
    )(in_hbm(mine), in_hbm(other), root, far_root)
    arrived = lax.all_to_all(precond, "x", 0, 0, tiled=True)
    shape = jax.ShapeDtypeStruct((ROWS, BS), F32)
    outs = call(
        factor_kernel, (shape,) * 4, [ANY] * 2 + [HBM] * 4 + [ANY] * 2,
        scratch=[
            pltpu.VMEM((BS, BS), BF16),
            pltpu.VMEM((SIDE, BS), F32),
            pltpu.VMEM((4, ROWS, BS), F32),
            pltpu.VMEM((2, BS, BS), BF16),
            pltpu.SemaphoreType.DMA((4, 4)),
        ],
        flops=8 * 64 * 1024 * 1024, moved=8_000_000,
    )(in_hbm(mine), in_hbm(other), *map(in_hbm, (left_gram, right_gram, left_root, right_root)), fifth, far_fifth)
    return (*(o[None] for o in outs), arrived.astype(F32))


def solution(mesh):
    split = Mesh(mesh.devices.reshape(NZ, NC, NY, NX), (*TOK, *HID))
    factor = P(HID, TOK, None)
    return jax.shard_map(
        on_device,
        mesh=split,
        in_specs=(P(TOK, None), P(TOK, HID), factor, factor, factor, factor),
        out_specs=(factor, factor, factor, factor, P(None, TOK, HID)),
        check_vma=False,
    )
```

```python
import jax
import jax.numpy as jnp
from jax import lax
from jax.experimental import pallas as pl
from jax.experimental.pallas import tpu as pltpu
from jax.sharding import Mesh
from jax.sharding import PartitionSpec as P

BETA = 0.95
EPS = 1e-06
F32 = jnp.float32
BF16 = jnp.bfloat16
NZ, NC, NY, NX = 8, 2, 8, 4
BS = 1024
HALF = BS // NC
TOKENS = 128
ROWS = BS // (NZ * NC)
WIDTH = BS // NX
COT = NX * HALF
ROOT = COT + WIDTH
TILE = 512
SIDE = NC * ROWS
OFF = 3
SLABS = NX * ROWS
STRIP = (OFF + 2) * SIDE
TOK = ("z", "core")
HID = ("y", "x")
SWAP = [(0, 1), (1, 0)]
VMEM = pl.BlockSpec(memory_space=pltpu.VMEM)
ANY = pl.BlockSpec(memory_space=pl.ANY)
HBM = pl.BlockSpec(memory_space=pltpu.HBM)
PARAMS = pltpu.CompilerParams(vmem_limit_bytes=28 * 1024 * 1024)


def dot(a, b, dims=((1,), (0,))):
    return lax.dot_general(a, b, (dims, ((), ())), preferred_element_type=F32)


def call(body, outs, specs, scratch=(), flops=0, moved=0, places=None):
    return pl.pallas_call(
        body,
        out_shape=outs,
        in_specs=specs,
        out_specs=places or jax.tree.map(lambda _: VMEM, outs),
        scratch_shapes=list(scratch),
        compiler_params=PARAMS,
        cost_estimate=pl.CostEstimate(flops=flops, bytes_accessed=moved, transcendentals=0),
    )


def in_hbm(value):
    return pltpu.with_memory_space_constraint(value, pltpu.HBM)


def at(start, size, unit):
    return pl.ds(pl.multiple_of(start, unit), size)


def pack_kernel(act, cot, left_root, right_root, own, far, roots, sems):
    core = lax.axis_index("core")
    copies = []
    for k, (out, side) in enumerate(((far, 1 - core), (own, core))):
        for r in range(NX):
            source = act.at[:, at(r * BS + side * HALF, HALF, 128)]
            target = out.at[:, pl.ds(r * HALF, HALF)]
            copies.append(pltpu.make_async_copy(source, target, sems.at[k, r]))
        copies.append(pltpu.make_async_copy(cot, out.at[:, pl.ds(COT, WIDTH)], sems.at[k, NX]))
    copies.append(pltpu.make_async_copy(left_root, roots.at[0], sems.at[0, NX + 1]))
    copies.append(pltpu.make_async_copy(right_root, roots.at[1], sems.at[1, NX + 1]))
    for copy in copies:
        copy.start()
    for copy in copies:
        copy.wait()
    for out, side in ((far, 1 - core), (own, core)):
        low = roots[side].astype(BF16)
        out[:ROWS, ROOT:] = low[:, :HALF]
        out[ROWS:, ROOT:] = low[:, HALF:]


def strip_kernel(own, more, strip, shard):
    z, core = lax.axis_index("z"), lax.axis_index("core")
    for given, side in ((own, core), (more, 1 - core)):
        rows = at(side * ROWS, ROWS, ROWS)
        shard[rows, :HALF] = given[:ROWS, ROOT:]
        shard[rows, HALF:] = given[ROWS:, ROOT:]
    for k in range(OFF + 2):
        strip[:, k * SIDE : (k + 1) * SIDE] = shard[:, at(lax.rem(z + k, NZ) * SIDE, SIDE, SIDE)]


def partial_kernel(own, more, out):
    for r in range(NX):
        cols = slice(r * HALF, (r + 1) * HALF)
        total = dot(own[:, cols], own[:, COT : COT + WIDTH], ((0,), (0,)))
        total += dot(more[:, cols], more[:, COT : COT + WIDTH], ((0,), (0,)))
        low = total.astype(BF16)
        for to in range(NZ):
            out[to, r * ROWS : (r + 1) * ROWS] = low[to * ROWS : (to + 1) * ROWS]


def sum_kernel(parts, out):
    for x in range(NX):
        rows = slice(x * ROWS, (x + 1) * ROWS)
        total = parts[0, rows].astype(F32)
        for z in range(1, NZ):
            total += parts[z, rows].astype(F32)
        low = total.astype(BF16)
        for z in range(NZ):
            out[x, z] = low


def root_kernel(strips, root):
    for z in range(NZ):
        own = slice(z * SIDE, (z + 1) * SIDE)
        for k in range(OFF + 2):
            j = (z + k) % NZ
            there = slice(j * SIDE, (j + 1) * SIDE)
            piece = strips[own, k * SIDE : (k + 1) * SIDE]
            root[own, there] = piece
            if 0 < k <= OFF:
                root[there, own] = piece.T


def precond_kernel(mine, other, root, far_root, out, stored, whole, left, right, kept, sems):
    z, core = lax.axis_index("z"), lax.axis_index("core")
    place = (z * NC + core) * ROWS

    def bring(first, second):
        return [
            pltpu.make_async_copy(first, left, sems.at[2, 0]),
            pltpu.make_async_copy(second, right, sems.at[2, 1]),
        ]

    pieces = []
    for k, (half, side) in enumerate(((mine, core), (other, 1 - core))):
        for x in range(NX):
            target = whole.at[at(side * HALF, HALF, HALF), pl.ds(x * WIDTH, WIDTH)]
            pieces.append(pltpu.make_async_copy(half.at[x], target, sems.at[k, x]))
    for copy in pieces:
        copy.start()

    @pl.when(core == 0)
    def _():
        for copy in bring(root, far_root):
            copy.start()

    @pl.when(core == 1)
    def _():
        for copy in bring(far_root, root):
            copy.start()

    for copy in pieces + bring(root, far_root):
        copy.wait()
    store = pltpu.make_async_copy(whole, stored, sems.at[2, 2])
    store.start()

    def tile(i, total):
        rows = at(i * TILE, TILE, TILE)
        precond = dot(dot(left[rows], whole[...]).astype(BF16), right[...])

        @pl.when(i == place // TILE)
        def _():
            kept[...] = precond

        return total + jnp.sum(precond * precond, axis=0, keepdims=True)

    total = lax.fori_loop(0, BS // TILE, tile, jnp.zeros((1, BS), F32))
    scale = 1.0 / jnp.sqrt(jnp.sum(total) / (BS * BS) + EPS)
    scaled = kept[at(place % TILE, ROWS, ROWS)] * scale
    for x in range(NX):
        out[x] = scaled[:, x * WIDTH : (x + 1) * WIDTH].astype(BF16)
    store.wait()


def factor_kernel(
    stored, left_gram, right_gram, left_root, right_root, root, far_root,
    left_next, right_next, left_refined, right_refined, whole, columns, old, powers, sems,
):
    z, core = lax.axis_index("z"), lax.axis_index("core")
    even = core == 0
    olds = [
        pltpu.make_async_copy(source, old.at[k], sems.at[0, k])
        for k, source in enumerate((left_gram, right_gram, left_root, right_root))
    ]
    both = [
        pltpu.make_async_copy(source, powers.at[k], sems.at[1, k])
        for k, source in enumerate((root, far_root))
    ]
    load = pltpu.make_async_copy(stored, whole, sems.at[2, 0])
    for copy in [load] + olds + both:
        copy.start()
    load.wait()
    slab = whole[:, at(z * SIDE, SIDE, SIDE)]
    columns[...] = slab.astype(F32).T
    rows = whole[at((z * NC + core) * ROWS, ROWS, ROWS)]
    left = dot(rows, whole[...], ((1,), (1,)))
    turned = columns[at(core * ROWS, ROWS, ROWS)].astype(BF16)
    right = dot(turned, whole[...])
    for copy in olds + both:
        copy.wait()
    left = BETA * old[0] + left
    left_next[...] = left
    right = BETA * old[1] + right
    right_next[...] = right
    own, far = jnp.where(even, left, right), jnp.where(even, right, left)
    for _ in range(5):
        own, far = dot(own.astype(BF16), powers[0]), dot(far.astype(BF16), powers[1])
    left_refined[...] = (5.0 * old[2] - jnp.where(even, own, far)) / 4.0
    right_refined[...] = (5.0 * old[3] - jnp.where(even, far, own)) / 4.0


def on_device(activations, cotangent, left_gram, right_gram, left_root, right_root):
    left_gram, right_gram = left_gram[0], right_gram[0]
    left_root, right_root = left_root[0], right_root[0]

    half = jax.ShapeDtypeStruct((TOKENS, ROOT + HALF), BF16)
    own, far = call(
        pack_kernel, (half, half), [HBM] * 4,
        scratch=[pltpu.VMEM((2, ROWS, BS), F32), pltpu.SemaphoreType.DMA((2, NX + 2))],
        flops=100_000, moved=1_500_000,
    )(*map(in_hbm, (activations, cotangent, left_root, right_root)))
    more = lax.ppermute(far, "core", SWAP)
    strip = call(
        strip_kernel, jax.ShapeDtypeStruct((SIDE, STRIP), BF16), [VMEM, VMEM],
        scratch=[pltpu.VMEM((SIDE, BS), BF16)], moved=500_000,
    )(own, more)
    strip, more = lax.optimization_barrier((strip, more))
    strips = lax.all_gather(strip, "z", axis=0, tiled=True)
    partial = call(
        partial_kernel, jax.ShapeDtypeStruct((NZ, SLABS, WIDTH), BF16), [VMEM, VMEM],
        flops=2 * 256 * 2048 * 256, moved=3_000_000,
    )(own, more)
    parts = lax.all_to_all(partial, "z", 0, 0, tiled=True)
    copies = call(
        sum_kernel, jax.ShapeDtypeStruct((NX, NZ, ROWS, WIDTH), BF16), [VMEM],
        flops=1_000_000, moved=2_000_000,
    )(parts)
    root = call(
        root_kernel, jax.ShapeDtypeStruct((BS, BS), BF16), [VMEM], flops=1_000_000, moved=4_000_000
    )(strips)
    far_root = lax.ppermute(root, "core", SWAP)
    mine = lax.all_to_all(
        copies.reshape(NX * NZ, ROWS, WIDTH), ("x", "z"), 0, 0, tiled=True
    ).reshape(NX, HALF, WIDTH)
    other = lax.ppermute(mine, "core", SWAP)

    square = jax.ShapeDtypeStruct((BS, BS), BF16)
    precond, whole = call(
        precond_kernel, (jax.ShapeDtypeStruct((NX, ROWS, WIDTH), BF16), square), [ANY] * 4,
        places=(VMEM, HBM),
        scratch=[
            pltpu.VMEM((BS, BS), BF16),
            pltpu.VMEM((BS, BS), BF16),
            pltpu.VMEM((BS, BS), BF16),
            pltpu.VMEM((TILE, BS), F32),
            pltpu.SemaphoreType.DMA((3, 4)),
        ],
        flops=4 * BS**3, moved=6_000_000,
    )(mine, other, root, far_root)
    arrived = lax.all_to_all(precond, "x", 0, 0, tiled=True)
    shape = jax.ShapeDtypeStruct((ROWS, BS), F32)
    outs = call(
        factor_kernel, (shape,) * 4, [HBM] * 5 + [ANY] * 2,
        scratch=[
            pltpu.VMEM((BS, BS), BF16),
            pltpu.VMEM((SIDE, BS), F32),
            pltpu.VMEM((4, ROWS, BS), F32),
            pltpu.VMEM((2, BS, BS), BF16),
            pltpu.SemaphoreType.DMA((3, 4)),
        ],
        flops=8 * 64 * 1024 * 1024, moved=8_000_000,
    )(*map(in_hbm, (whole, left_gram, right_gram, left_root, right_root)), root, far_root)
    return (*(o[None] for o in outs), arrived.astype(F32))


def solution(mesh):
    split = Mesh(mesh.devices.reshape(NZ, NC, NY, NX), (*TOK, *HID))
    factor = P(HID, TOK, None)
    return jax.shard_map(
        on_device,
        mesh=split,
        in_specs=(P(TOK, None), P(TOK, HID), factor, factor, factor, factor),
        out_specs=(factor, factor, factor, factor, P(None, TOK, HID)),
        check_vma=False,
    )
```

```python
import jax
import jax.numpy as jnp
from jax import lax
from jax.experimental import pallas as pl
from jax.experimental.pallas import tpu as pltpu
from jax.sharding import Mesh
from jax.sharding import PartitionSpec as P

BETA = 0.95
EPS = 1e-06
F32 = jnp.float32
BF16 = jnp.bfloat16
NZ, NC, NY, NX = 8, 2, 8, 4
BS = 1024
HALF = BS // NC
TOKENS = 128
ROWS = BS // (NZ * NC)
WIDTH = BS // NX
COT = NX * HALF
ROOT = COT + WIDTH
TILE = 512
SIDE = NC * ROWS
OFF = 3
SLABS = NX * ROWS
STRIP = (OFF + 2) * SIDE
TOK = ("z", "core")
HID = ("y", "x")
SWAP = [(0, 1), (1, 0)]
VMEM = pl.BlockSpec(memory_space=pltpu.VMEM)
ANY = pl.BlockSpec(memory_space=pl.ANY)
HBM = pl.BlockSpec(memory_space=pltpu.HBM)
PARAMS = pltpu.CompilerParams(vmem_limit_bytes=28 * 1024 * 1024)


def dot(a, b, dims=((1,), (0,))):
    return lax.dot_general(a, b, (dims, ((), ())), preferred_element_type=F32)


def call(body, outs, specs, scratch=(), flops=0, moved=0, places=None):
    return pl.pallas_call(
        body,
        out_shape=outs,
        in_specs=specs,
        out_specs=places or jax.tree.map(lambda _: VMEM, outs),
        scratch_shapes=list(scratch),
        compiler_params=PARAMS,
        cost_estimate=pl.CostEstimate(flops=flops, bytes_accessed=moved, transcendentals=0),
    )


def in_hbm(value):
    return pltpu.with_memory_space_constraint(value, pltpu.HBM)


def at(start, size, unit):
    return pl.ds(pl.multiple_of(start, unit), size)


def pack_kernel(act, cot, left_root, right_root, own, far, roots, sems):
    core = lax.axis_index("core")
    copies = []
    for k, (out, side) in enumerate(((far, 1 - core), (own, core))):
        for r in range(NX):
            source = act.at[:, at(r * BS + side * HALF, HALF, 128)]
            target = out.at[:, pl.ds(r * HALF, HALF)]
            copies.append(pltpu.make_async_copy(source, target, sems.at[k, r]))
        copies.append(pltpu.make_async_copy(cot, out.at[:, pl.ds(COT, WIDTH)], sems.at[k, NX]))
    copies.append(pltpu.make_async_copy(left_root, roots.at[0], sems.at[0, NX + 1]))
    copies.append(pltpu.make_async_copy(right_root, roots.at[1], sems.at[1, NX + 1]))
    for copy in copies:
        copy.start()
    for copy in copies:
        copy.wait()
    for out, side in ((far, 1 - core), (own, core)):
        low = roots[side].astype(BF16)
        out[:ROWS, ROOT:] = low[:, :HALF]
        out[ROWS:, ROOT:] = low[:, HALF:]


def strip_kernel(own, more, strip, shard):
    z, core = lax.axis_index("z"), lax.axis_index("core")
    for given, side in ((own, core), (more, 1 - core)):
        rows = at(side * ROWS, ROWS, ROWS)
        shard[rows, :HALF] = given[:ROWS, ROOT:]
        shard[rows, HALF:] = given[ROWS:, ROOT:]
    for k in range(OFF + 2):
        strip[:, k * SIDE : (k + 1) * SIDE] = shard[:, at(lax.rem(z + k, NZ) * SIDE, SIDE, SIDE)]


def partial_kernel(own, more, out):
    for r in range(NX):
        cols = slice(r * HALF, (r + 1) * HALF)
        total = dot(own[:, cols], own[:, COT : COT + WIDTH], ((0,), (0,)))
        total += dot(more[:, cols], more[:, COT : COT + WIDTH], ((0,), (0,)))
        low = total.astype(BF16)
        for to in range(NZ):
            out[to, r * ROWS : (r + 1) * ROWS] = low[to * ROWS : (to + 1) * ROWS]


def sum_kernel(parts, out):
    for x in range(NX):
        rows = slice(x * ROWS, (x + 1) * ROWS)
        total = parts[0, rows].astype(F32)
        for z in range(1, NZ):
            total += parts[z, rows].astype(F32)
        low = total.astype(BF16)
        for z in range(NZ):
            out[x, z] = low


def root_kernel(strips, root):
    for z in range(NZ):
        own = slice(z * SIDE, (z + 1) * SIDE)
        for k in range(OFF + 2):
            j = (z + k) % NZ
            there = slice(j * SIDE, (j + 1) * SIDE)
            piece = strips[own, k * SIDE : (k + 1) * SIDE]
            root[own, there] = piece
            if 0 < k <= OFF:
                root[there, own] = piece.T


def precond_kernel(mine, other, root, far_root, out, stored, whole, left, right, kept, sems):
    z, core = lax.axis_index("z"), lax.axis_index("core")
    place = (z * NC + core) * ROWS

    def bring(first, second):
        return [
            pltpu.make_async_copy(first, left, sems.at[2, 0]),
            pltpu.make_async_copy(second, right, sems.at[2, 1]),
        ]

    pieces = []
    for k, (half, side) in enumerate(((mine, core), (other, 1 - core))):
        for x in range(NX):
            target = whole.at[at(side * HALF, HALF, HALF), pl.ds(x * WIDTH, WIDTH)]
            pieces.append(pltpu.make_async_copy(half.at[x], target, sems.at[k, x]))
    for copy in pieces:
        copy.start()

    @pl.when(core == 0)
    def _():
        for copy in bring(root, far_root):
            copy.start()

    @pl.when(core == 1)
    def _():
        for copy in bring(far_root, root):
            copy.start()

    applies, follows = bring(root, far_root)
    for copy in pieces + [applies]:
        copy.wait()
    store = pltpu.make_async_copy(whole, stored, sems.at[2, 2])
    store.start()

    total = jnp.zeros((1, BS), F32)
    for i in range(BS // TILE):
        applied = dot(left[i * TILE : (i + 1) * TILE], whole[...]).astype(BF16)
        if i == 0:
            follows.wait()
        precond = dot(applied, right[...])
        total += jnp.sum(precond * precond, axis=0, keepdims=True)

        @pl.when(i == place // TILE)
        def _(precond=precond):
            kept[...] = precond

    scale = 1.0 / jnp.sqrt(jnp.sum(total) / (BS * BS) + EPS)
    scaled = kept[at(place % TILE, ROWS, ROWS)] * scale
    for x in range(NX):
        out[x] = scaled[:, x * WIDTH : (x + 1) * WIDTH].astype(BF16)
    store.wait()


def square_kernel(root, squared):
    for i in range(0, BS, TILE):
        squared[i : i + TILE] = dot(root[i : i + TILE], root[...]).astype(BF16)


def factor_kernel(
    stored, left_gram, right_gram, left_root, right_root, squared, far_squared, root, far_root,
    left_next, right_next, left_refined, right_refined, whole, columns, old, powers, sems,
):
    z, core = lax.axis_index("z"), lax.axis_index("core")
    even = core == 0
    olds = [
        pltpu.make_async_copy(source, old.at[k], sems.at[0, k])
        for k, source in enumerate((left_gram, right_gram, left_root, right_root))
    ]
    both = [
        pltpu.make_async_copy(source, powers.at[k], sems.at[1, k])
        for k, source in enumerate((squared, far_squared, root, far_root))
    ]
    load = pltpu.make_async_copy(stored, whole, sems.at[2, 0])
    for copy in [load] + olds + both:
        copy.start()
    load.wait()
    slab = whole[:, at(z * SIDE, SIDE, SIDE)]
    columns[...] = slab.astype(F32).T
    rows = whole[at((z * NC + core) * ROWS, ROWS, ROWS)]
    left = dot(rows, whole[...], ((1,), (1,)))
    turned = columns[at(core * ROWS, ROWS, ROWS)].astype(BF16)
    right = dot(turned, whole[...])
    for copy in olds + both[:2]:
        copy.wait()
    left = BETA * old[0] + left
    left_next[...] = left
    right = BETA * old[1] + right
    right_next[...] = right
    own, far = jnp.where(even, left, right), jnp.where(even, right, left)
    for _ in range(2):
        own, far = dot(own.astype(BF16), powers[0]), dot(far.astype(BF16), powers[1])
    for copy in both[2:]:
        copy.wait()
    own, far = dot(own.astype(BF16), powers[2]), dot(far.astype(BF16), powers[3])
    left_refined[...] = (5.0 * old[2] - jnp.where(even, own, far)) / 4.0
    right_refined[...] = (5.0 * old[3] - jnp.where(even, far, own)) / 4.0


def on_device(activations, cotangent, left_gram, right_gram, left_root, right_root):
    left_gram, right_gram = left_gram[0], right_gram[0]
    left_root, right_root = left_root[0], right_root[0]

    half = jax.ShapeDtypeStruct((TOKENS, ROOT + HALF), BF16)
    own, far = call(
        pack_kernel, (half, half), [HBM] * 4,
        scratch=[pltpu.VMEM((2, ROWS, BS), F32), pltpu.SemaphoreType.DMA((2, NX + 2))],
        flops=100_000, moved=1_500_000,
    )(*map(in_hbm, (activations, cotangent, left_root, right_root)))
    more = lax.ppermute(far, "core", SWAP)
    strip = call(
        strip_kernel, jax.ShapeDtypeStruct((SIDE, STRIP), BF16), [VMEM, VMEM],
        scratch=[pltpu.VMEM((SIDE, BS), BF16)], moved=500_000,
    )(own, more)
    strip, more = lax.optimization_barrier((strip, more))
    strips = lax.all_gather(strip, "z", axis=0, tiled=True)
    partial = call(
        partial_kernel, jax.ShapeDtypeStruct((NZ, SLABS, WIDTH), BF16), [VMEM, VMEM],
        flops=2 * 256 * 2048 * 256, moved=3_000_000,
    )(own, more)
    parts = lax.all_to_all(partial, "z", 0, 0, tiled=True)
    copies = call(
        sum_kernel, jax.ShapeDtypeStruct((NX, NZ, ROWS, WIDTH), BF16), [VMEM],
        flops=1_000_000, moved=2_000_000,
    )(parts)
    root = call(
        root_kernel, jax.ShapeDtypeStruct((BS, BS), BF16), [VMEM], flops=1_000_000, moved=4_000_000
    )(strips)
    far_root = lax.ppermute(root, "core", SWAP)
    squared = call(
        square_kernel, jax.ShapeDtypeStruct((BS, BS), BF16), [VMEM], flops=2 * BS**3, moved=4_000_000
    )(root)
    far_squared = lax.ppermute(squared, "core", SWAP)
    mine = lax.all_to_all(
        copies.reshape(NX * NZ, ROWS, WIDTH), ("x", "z"), 0, 0, tiled=True
    ).reshape(NX, HALF, WIDTH)
    other = lax.ppermute(mine, "core", SWAP)

    square = pltpu.HBM((BS, BS), BF16)
    precond, whole = call(
        precond_kernel, (jax.ShapeDtypeStruct((NX, ROWS, WIDTH), BF16), square), [ANY] * 4,
        places=(VMEM, HBM),
        scratch=[
            pltpu.VMEM((BS, BS), BF16),
            pltpu.VMEM((BS, BS), BF16),
            pltpu.VMEM((BS, BS), BF16),
            pltpu.VMEM((TILE, BS), F32),
            pltpu.SemaphoreType.DMA((3, 4)),
        ],
        flops=4 * BS**3, moved=6_000_000,
    )(mine, other, root, far_root)
    arrived = lax.all_to_all(precond, "x", 0, 0, tiled=True)
    shape = jax.ShapeDtypeStruct((ROWS, BS), F32)
    outs = call(
        factor_kernel, (shape,) * 4, [HBM] * 5 + [ANY] * 4,
        scratch=[
            pltpu.VMEM((BS, BS), BF16),
            pltpu.VMEM((SIDE, BS), F32),
            pltpu.VMEM((4, ROWS, BS), F32),
            pltpu.VMEM((4, BS, BS), BF16),
            pltpu.SemaphoreType.DMA((3, 4)),
        ],
        flops=16 * 64 * 1024 * 1024, moved=8_000_000,
    )(*map(in_hbm, (whole, left_gram, right_gram, left_root, right_root)), squared, far_squared, root, far_root)
    return (*(o[None] for o in outs), arrived.astype(F32))


def solution(mesh):
    split = Mesh(mesh.devices.reshape(NZ, NC, NY, NX), (*TOK, *HID))
    factor = P(HID, TOK, None)
    return jax.shard_map(
        on_device,
        mesh=split,
        in_specs=(P(TOK, None), P(TOK, HID), factor, factor, factor, factor),
        out_specs=(factor, factor, factor, factor, P(None, TOK, HID)),
        check_vma=False,
    )
```

```python
import functools

import jax
import jax.numpy as jnp
from jax import lax
from jax.experimental import pallas as pl
from jax.experimental.pallas import tpu as pltpu
from jax.sharding import Mesh
from jax.sharding import PartitionSpec as P

BETA = 0.95
EPS = 1e-06
F32 = jnp.float32
BF16 = jnp.bfloat16
NZ, NC, NY, NX = 8, 2, 8, 4
BS = 1024
HALF = BS // NC
TOKENS = 128
ROWS = BS // (NZ * NC)
WIDTH = BS // NX
COT = NX * HALF
ROOT = COT + WIDTH
TILE = 512
SIDE = NC * ROWS
OFF = 3
SLABS = NX * ROWS
STRIP = (OFF + 2) * SIDE
TOK = ("z", "core")
HID = ("y", "x")
SWAP = [(0, 1), (1, 0)]
VMEM = pl.BlockSpec(memory_space=pltpu.VMEM)
ANY = pl.BlockSpec(memory_space=pl.ANY)
HBM = pl.BlockSpec(memory_space=pltpu.HBM)
PARAMS = pltpu.CompilerParams(vmem_limit_bytes=28 * 1024 * 1024)


def dot(a, b, dims=((1,), (0,))):
    return lax.dot_general(a, b, (dims, ((), ())), preferred_element_type=F32)


def call(body, outs, specs, scratch=(), flops=0, moved=0, places=None):
    return pl.pallas_call(
        body,
        out_shape=outs,
        in_specs=specs,
        out_specs=places or jax.tree.map(lambda _: VMEM, outs),
        scratch_shapes=list(scratch),
        compiler_params=PARAMS,
        cost_estimate=pl.CostEstimate(flops=flops, bytes_accessed=moved, transcendentals=0),
    )


def in_hbm(value):
    return pltpu.with_memory_space_constraint(value, pltpu.HBM)


def at(start, size, unit):
    return pl.ds(pl.multiple_of(start, unit), size)


def pack_kernel(mate, act, cot, left_root, right_root, out, root, sems):
    core = lax.axis_index("core")
    side = 1 - core if mate else core
    copies = [pltpu.make_async_copy(cot, out.at[:, pl.ds(COT, WIDTH)], sems.at[NX])]
    for r in range(NX):
        source = act.at[:, at(r * BS + side * HALF, HALF, 128)]
        copies.append(pltpu.make_async_copy(source, out.at[:, pl.ds(r * HALF, HALF)], sems.at[r]))
    for k, source in enumerate((left_root, right_root)):

        @pl.when(side == k)
        def _(source=source):
            pltpu.make_async_copy(source, root, sems.at[NX + 1]).start()

    for copy in copies:
        copy.start()
    pltpu.make_async_copy(left_root, root, sems.at[NX + 1]).wait()
    low = root[...].astype(BF16)
    out[:ROWS, ROOT:] = low[:, :HALF]
    out[ROWS:, ROOT:] = low[:, HALF:]
    for copy in copies:
        copy.wait()


def strip_kernel(own, more, strip, shard):
    z, core = lax.axis_index("z"), lax.axis_index("core")
    for given, side in ((own, core), (more, 1 - core)):
        rows = at(side * ROWS, ROWS, ROWS)
        shard[rows, :HALF] = given[:ROWS, ROOT:]
        shard[rows, HALF:] = given[ROWS:, ROOT:]
    for k in range(OFF + 2):
        strip[:, k * SIDE : (k + 1) * SIDE] = shard[:, at(lax.rem(z + k, NZ) * SIDE, SIDE, SIDE)]


def partial_kernel(own, more, out):
    for r in range(NX):
        cols = slice(r * HALF, (r + 1) * HALF)
        total = dot(own[:, cols], own[:, COT : COT + WIDTH], ((0,), (0,)))
        total += dot(more[:, cols], more[:, COT : COT + WIDTH], ((0,), (0,)))
        low = total.astype(BF16)
        for to in range(NZ):
            out[to, r * ROWS : (r + 1) * ROWS] = low[to * ROWS : (to + 1) * ROWS]


def sum_kernel(parts, out):
    for x in range(NX):
        rows = slice(x * ROWS, (x + 1) * ROWS)
        total = parts[0, rows].astype(F32)
        for z in range(1, NZ):
            total += parts[z, rows].astype(F32)
        low = total.astype(BF16)
        for z in range(NZ):
            out[x, z] = low


def root_kernel(strips, root):
    for z in range(NZ):
        own = slice(z * SIDE, (z + 1) * SIDE)
        for k in range(OFF + 2):
            j = (z + k) % NZ
            there = slice(j * SIDE, (j + 1) * SIDE)
            piece = strips[own, k * SIDE : (k + 1) * SIDE]
            root[own, there] = piece
            if 0 < k <= OFF:
                root[there, own] = piece.T


def first_kernel(mine, root, far_root, out, upper, left, sems):
    core = lax.axis_index("core")
    cols = at(core * HALF, HALF, 128)
    pieces = [
        pltpu.make_async_copy(mine.at[x], upper.at[:, pl.ds(x * WIDTH, WIDTH)], sems.at[x])
        for x in range(NX)
    ]
    for copy in pieces:
        copy.start()
    for side, source in enumerate((root, far_root)):

        @pl.when(core == side)
        def _(source=source):
            pltpu.make_async_copy(source.at[:, cols], left, sems.at[NX]).start()

    for copy in pieces + [pltpu.make_async_copy(root.at[:, cols], left, sems.at[NX])]:
        copy.wait()
    for i in range(0, BS, TILE):
        out[i : i + TILE] = dot(left[i : i + TILE], upper[...])


def precond_kernel(
    mine, other, root, far_root, first, out, stored, whole, left, right, kept, sems
):
    z, core = lax.axis_index("z"), lax.axis_index("core")
    place = (z * NC + core) * ROWS

    cols = at((1 - core) * HALF, HALF, 128)

    def bring(applied_by, second):
        return [
            pltpu.make_async_copy(applied_by.at[:, cols], left, sems.at[2, 0]),
            pltpu.make_async_copy(second, right, sems.at[2, 1]),
        ]

    pieces = []
    for k, (half, side) in enumerate(((mine, core), (other, 1 - core))):
        for x in range(NX):
            target = whole.at[at(side * HALF, HALF, HALF), pl.ds(x * WIDTH, WIDTH)]
            pieces.append(pltpu.make_async_copy(half.at[x], target, sems.at[k, x]))
    for copy in pieces:
        copy.start()

    @pl.when(core == 0)
    def _():
        for copy in bring(root, far_root):
            copy.start()

    @pl.when(core == 1)
    def _():
        for copy in bring(far_root, root):
            copy.start()

    applies, follows = bring(root, far_root)
    for copy in pieces + [applies]:
        copy.wait()
    store = pltpu.make_async_copy(whole, stored, sems.at[2, 2])
    store.start()

    total = jnp.zeros((1, BS), F32)
    for i in range(BS // TILE):
        part = slice(i * TILE, (i + 1) * TILE)
        lower = whole[at((1 - core) * HALF, HALF, HALF)]
        applied = (first[part] + dot(left[part], lower)).astype(BF16)
        if i == 0:
            follows.wait()
        precond = dot(applied, right[...])
        total += jnp.sum(precond * precond, axis=0, keepdims=True)

        @pl.when(i == place // TILE)
        def _(precond=precond):
            kept[...] = precond

    scale = 1.0 / jnp.sqrt(jnp.sum(total) / (BS * BS) + EPS)
    scaled = kept[at(place % TILE, ROWS, ROWS)] * scale
    for x in range(NX):
        out[x] = scaled[:, x * WIDTH : (x + 1) * WIDTH].astype(BF16)
    store.wait()


def square_kernel(root, squared):
    for i in range(0, BS, TILE):
        squared[i : i + TILE] = dot(root[i : i + TILE], root[...]).astype(BF16)


def factor_kernel(
    stored, left_gram, right_gram, left_root, right_root, squared, far_squared, root, far_root,
    left_next, right_next, left_refined, right_refined, whole, columns, old, powers, sems,
):
    z, core = lax.axis_index("z"), lax.axis_index("core")
    even = core == 0
    olds = [
        pltpu.make_async_copy(source, old.at[k], sems.at[0, k])
        for k, source in enumerate((left_gram, right_gram, left_root, right_root))
    ]
    both = [
        pltpu.make_async_copy(source, powers.at[k], sems.at[1, k])
        for k, source in enumerate((squared, far_squared, root, far_root))
    ]
    load = pltpu.make_async_copy(stored, whole, sems.at[2, 0])
    for copy in [load] + olds + both:
        copy.start()
    load.wait()
    slab = whole[:, at(z * SIDE, SIDE, SIDE)]
    columns[...] = slab.astype(F32).T
    rows = whole[at((z * NC + core) * ROWS, ROWS, ROWS)]
    left = dot(rows, whole[...], ((1,), (1,)))
    turned = columns[at(core * ROWS, ROWS, ROWS)].astype(BF16)
    right = dot(turned, whole[...])
    for copy in olds + both[:2]:
        copy.wait()
    left = BETA * old[0] + left
    left_next[...] = left
    right = BETA * old[1] + right
    right_next[...] = right
    own, far = jnp.where(even, left, right), jnp.where(even, right, left)
    for _ in range(2):
        own, far = dot(own.astype(BF16), powers[0]), dot(far.astype(BF16), powers[1])
    for copy in both[2:]:
        copy.wait()
    own, far = dot(own.astype(BF16), powers[2]), dot(far.astype(BF16), powers[3])
    left_refined[...] = (5.0 * old[2] - jnp.where(even, own, far)) / 4.0
    right_refined[...] = (5.0 * old[3] - jnp.where(even, far, own)) / 4.0


def on_device(activations, cotangent, left_gram, right_gram, left_root, right_root):
    left_gram, right_gram = left_gram[0], right_gram[0]
    left_root, right_root = left_root[0], right_root[0]

    def pack(mate):
        return call(
            functools.partial(pack_kernel, mate),
            jax.ShapeDtypeStruct((TOKENS, ROOT + HALF), BF16), [HBM] * 4,
            scratch=[pltpu.VMEM((ROWS, BS), F32), pltpu.SemaphoreType.DMA((NX + 2,))],
            flops=100_000, moved=1_000_000,
        )(*map(in_hbm, (activations, cotangent, left_root, right_root)))

    far = pack(1)
    more = lax.ppermute(far, "core", SWAP)
    own = pack(0)
    more, own = lax.optimization_barrier((more, own))
    strip = call(
        strip_kernel, jax.ShapeDtypeStruct((SIDE, STRIP), BF16), [VMEM, VMEM],
        scratch=[pltpu.VMEM((SIDE, BS), BF16)], moved=500_000,
    )(own, more)
    strip, more = lax.optimization_barrier((strip, more))
    strips = lax.all_gather(strip, "z", axis=0, tiled=True)
    partial = call(
        partial_kernel, jax.ShapeDtypeStruct((NZ, SLABS, WIDTH), BF16), [VMEM, VMEM],
        flops=2 * 256 * 2048 * 256, moved=3_000_000,
    )(own, more)
    parts = lax.all_to_all(partial, "z", 0, 0, tiled=True)
    copies = call(
        sum_kernel, jax.ShapeDtypeStruct((NX, NZ, ROWS, WIDTH), BF16), [VMEM],
        flops=1_000_000, moved=2_000_000,
    )(parts)
    root = call(
        root_kernel, jax.ShapeDtypeStruct((BS, BS), BF16), [VMEM], flops=1_000_000, moved=4_000_000
    )(strips)
    far_root = lax.ppermute(root, "core", SWAP)
    squared = call(
        square_kernel, jax.ShapeDtypeStruct((BS, BS), BF16), [VMEM], flops=2 * BS**3, moved=4_000_000
    )(root)
    far_squared = lax.ppermute(squared, "core", SWAP)
    mine = lax.all_to_all(
        copies.reshape(NX * NZ, ROWS, WIDTH), ("x", "z"), 0, 0, tiled=True
    ).reshape(NX, HALF, WIDTH)
    other = lax.ppermute(mine, "core", SWAP)

    first = call(
        first_kernel, jax.ShapeDtypeStruct((BS, BS), F32), [ANY] * 3,
        scratch=[
            pltpu.VMEM((HALF, BS), BF16),
            pltpu.VMEM((BS, HALF), BF16),
            pltpu.SemaphoreType.DMA((NX + 1,)),
        ],
        flops=BS**3, moved=3_000_000,
    )(mine, root, far_root)
    other, first = lax.optimization_barrier((other, first))
    square = pltpu.HBM((BS, BS), BF16)
    precond, whole = call(
        precond_kernel, (jax.ShapeDtypeStruct((NX, ROWS, WIDTH), BF16), square), [ANY] * 4 + [VMEM],
        places=(VMEM, HBM),
        scratch=[
            pltpu.VMEM((BS, BS), BF16),
            pltpu.VMEM((BS, HALF), BF16),
            pltpu.VMEM((BS, BS), BF16),
            pltpu.VMEM((TILE, BS), F32),
            pltpu.SemaphoreType.DMA((3, 4)),
        ],
        flops=4 * BS**3, moved=6_000_000,
    )(mine, other, root, far_root, first)
    arrived = lax.all_to_all(precond, "x", 0, 0, tiled=True)
    shape = jax.ShapeDtypeStruct((ROWS, BS), F32)
    outs = call(
        factor_kernel, (shape,) * 4, [HBM] * 5 + [ANY] * 4,
        scratch=[
            pltpu.VMEM((BS, BS), BF16),
            pltpu.VMEM((SIDE, BS), F32),
            pltpu.VMEM((4, ROWS, BS), F32),
            pltpu.VMEM((4, BS, BS), BF16),
            pltpu.SemaphoreType.DMA((3, 4)),
        ],
        flops=16 * 64 * 1024 * 1024, moved=8_000_000,
    )(*map(in_hbm, (whole, left_gram, right_gram, left_root, right_root)), squared, far_squared, root, far_root)
    return (*(o[None] for o in outs), arrived.astype(F32))


def solution(mesh):
    split = Mesh(mesh.devices.reshape(NZ, NC, NY, NX), (*TOK, *HID))
    factor = P(HID, TOK, None)
    return jax.shard_map(
        on_device,
        mesh=split,
        in_specs=(P(TOK, None), P(TOK, HID), factor, factor, factor, factor),
        out_specs=(factor, factor, factor, factor, P(None, TOK, HID)),
        check_vma=False,
    )
```

```python
import functools

import jax
import jax.numpy as jnp
from jax import lax
from jax.experimental import pallas as pl
from jax.experimental.pallas import tpu as pltpu
from jax.sharding import Mesh
from jax.sharding import PartitionSpec as P

BETA = 0.95
EPS = 1e-06
F32 = jnp.float32
BF16 = jnp.bfloat16
NZ, NC, NY, NX = 8, 2, 8, 4
BS = 1024
HALF = BS // NC
TOKENS = 128
ROWS = BS // (NZ * NC)
WIDTH = BS // NX
COT = NX * HALF
ROOT = COT + WIDTH
TILE = 512
SIDE = NC * ROWS
OFF = 3
SLABS = NX * ROWS
STRIP = (OFF + 1) * SIDE
EXTRA = ROWS * SIDE // STRIP
TALL = SIDE + EXTRA
TOK = ("z", "core")
HID = ("y", "x")
SWAP = [(0, 1), (1, 0)]
VMEM = pl.BlockSpec(memory_space=pltpu.VMEM)
ANY = pl.BlockSpec(memory_space=pl.ANY)
HBM = pl.BlockSpec(memory_space=pltpu.HBM)
PARAMS = pltpu.CompilerParams(vmem_limit_bytes=28 * 1024 * 1024)


def dot(a, b, dims=((1,), (0,))):
    return lax.dot_general(a, b, (dims, ((), ())), preferred_element_type=F32)


def call(body, outs, specs, scratch=(), flops=0, moved=0, places=None):
    return pl.pallas_call(
        body,
        out_shape=outs,
        in_specs=specs,
        out_specs=places or jax.tree.map(lambda _: VMEM, outs),
        scratch_shapes=list(scratch),
        compiler_params=PARAMS,
        cost_estimate=pl.CostEstimate(flops=flops, bytes_accessed=moved, transcendentals=0),
    )


def in_hbm(value):
    return pltpu.with_memory_space_constraint(value, pltpu.HBM)


def at(start, size, unit):
    return pl.ds(pl.multiple_of(start, unit), size)


def pack_kernel(mate, act, cot, left_root, right_root, out, root, sems):
    core = lax.axis_index("core")
    side = 1 - core if mate else core
    copies = [pltpu.make_async_copy(cot, out.at[:, pl.ds(COT, WIDTH)], sems.at[NX])]
    for r in range(NX):
        source = act.at[:, at(r * BS + side * HALF, HALF, 128)]
        copies.append(pltpu.make_async_copy(source, out.at[:, pl.ds(r * HALF, HALF)], sems.at[r]))
    for k, source in enumerate((left_root, right_root)):

        @pl.when(side == k)
        def _(source=source):
            pltpu.make_async_copy(source, root, sems.at[NX + 1]).start()

    for copy in copies:
        copy.start()
    pltpu.make_async_copy(left_root, root, sems.at[NX + 1]).wait()
    low = root[...].astype(BF16)
    out[:ROWS, ROOT:] = low[:, :HALF]
    out[ROWS:, ROOT:] = low[:, HALF:]
    for copy in copies:
        copy.wait()


def strip_kernel(own, more, strip, shard):
    z, core = lax.axis_index("z"), lax.axis_index("core")
    for given, side in ((own, core), (more, 1 - core)):
        rows = at(side * ROWS, ROWS, ROWS)
        shard[rows, :HALF] = given[:ROWS, ROOT:]
        shard[rows, HALF:] = given[ROWS:, ROOT:]
    def block(k):
        return shard[:, at(lax.rem(z + k, NZ) * SIDE, SIDE, SIDE)]

    for k in range(OFF + 1):
        strip[:SIDE, k * SIDE : (k + 1) * SIDE] = block(k)

    across = block(OFF + 1).astype(F32)
    half = jnp.where(z < NZ // 2, across.T[:ROWS], across[ROWS:]).astype(BF16)
    for k in range(OFF + 1):
        strip[SIDE:, k * SIDE : (k + 1) * SIDE] = half[k * EXTRA : (k + 1) * EXTRA]


def partial_kernel(own, more, out):
    for r in range(NX):
        cols = slice(r * HALF, (r + 1) * HALF)
        total = dot(own[:, cols], own[:, COT : COT + WIDTH], ((0,), (0,)))
        total += dot(more[:, cols], more[:, COT : COT + WIDTH], ((0,), (0,)))
        low = total.astype(BF16)
        for to in range(NZ):
            out[to, r * ROWS : (r + 1) * ROWS] = low[to * ROWS : (to + 1) * ROWS]


def sum_kernel(parts, out):
    for x in range(NX):
        rows = slice(x * ROWS, (x + 1) * ROWS)
        total = parts[0, rows].astype(F32)
        for z in range(1, NZ):
            total += parts[z, rows].astype(F32)
        low = total.astype(BF16)
        for z in range(NZ):
            out[x, z] = low


def root_kernel(strips, root):
    def cut(z):
        return slice(z * SIDE, (z + 1) * SIDE)

    for z in range(NZ):
        for k in range(OFF + 1):
            there = cut((z + k) % NZ)
            piece = strips[z * TALL : z * TALL + SIDE, k * SIDE : (k + 1) * SIDE]
            root[cut(z), there] = piece
            if k:
                root[there, cut(z)] = piece.T
    for z in range(NZ // 2):
        pieces = [
            strips[home * TALL + SIDE : (home + 1) * TALL, k * SIDE : (k + 1) * SIDE]
            for home in (z, z + NZ // 2)
            for k in range(OFF + 1)
        ]
        whole = jnp.concatenate(pieces, axis=0)
        root[cut(z + NZ // 2), cut(z)] = whole
        root[cut(z), cut(z + NZ // 2)] = whole.T


def first_kernel(mine, root, far_root, out, upper, left, sems):
    core = lax.axis_index("core")
    cols = at(core * HALF, HALF, 128)
    pieces = [
        pltpu.make_async_copy(mine.at[x], upper.at[:, pl.ds(x * WIDTH, WIDTH)], sems.at[x])
        for x in range(NX)
    ]
    for copy in pieces:
        copy.start()
    for side, source in enumerate((root, far_root)):

        @pl.when(core == side)
        def _(source=source):
            pltpu.make_async_copy(source.at[:, cols], left, sems.at[NX]).start()

    for copy in pieces + [pltpu.make_async_copy(root.at[:, cols], left, sems.at[NX])]:
        copy.wait()
    for i in range(0, BS, TILE):
        out[i : i + TILE] = dot(left[i : i + TILE], upper[...])


def precond_kernel(
    mine, other, root, far_root, first, out, stored, whole, left, right, kept, sems
):
    z, core = lax.axis_index("z"), lax.axis_index("core")
    place = (z * NC + core) * ROWS

    cols = at((1 - core) * HALF, HALF, 128)

    def bring(applied_by, second):
        return [
            pltpu.make_async_copy(applied_by.at[:, cols], left, sems.at[2, 0]),
            pltpu.make_async_copy(second, right, sems.at[2, 1]),
        ]

    pieces = []
    for k, (half, side) in enumerate(((mine, core), (other, 1 - core))):
        for x in range(NX):
            target = whole.at[at(side * HALF, HALF, HALF), pl.ds(x * WIDTH, WIDTH)]
            pieces.append(pltpu.make_async_copy(half.at[x], target, sems.at[k, x]))
    for copy in pieces:
        copy.start()

    @pl.when(core == 0)
    def _():
        for copy in bring(root, far_root):
            copy.start()

    @pl.when(core == 1)
    def _():
        for copy in bring(far_root, root):
            copy.start()

    applies, follows = bring(root, far_root)
    for copy in pieces + [applies]:
        copy.wait()
    store = pltpu.make_async_copy(whole, stored, sems.at[2, 2])
    store.start()

    total = jnp.zeros((1, BS), F32)
    for i in range(BS // TILE):
        part = slice(i * TILE, (i + 1) * TILE)
        lower = whole[at((1 - core) * HALF, HALF, HALF)]
        applied = (first[part] + dot(left[part], lower)).astype(BF16)
        if i == 0:
            follows.wait()
        precond = dot(applied, right[...])
        total += jnp.sum(precond * precond, axis=0, keepdims=True)

        @pl.when(i == place // TILE)
        def _(precond=precond):
            kept[...] = precond

    scale = 1.0 / jnp.sqrt(jnp.sum(total) / (BS * BS) + EPS)
    scaled = kept[at(place % TILE, ROWS, ROWS)] * scale
    for x in range(NX):
        out[x] = scaled[:, x * WIDTH : (x + 1) * WIDTH].astype(BF16)
    store.wait()


def square_kernel(root, squared):
    for i in range(0, BS, TILE):
        squared[i : i + TILE] = dot(root[i : i + TILE], root[...]).astype(BF16)


def factor_kernel(
    stored, left_gram, right_gram, left_root, right_root, squared, far_squared, root, far_root,
    left_next, right_next, left_refined, right_refined, whole, columns, old, powers, sems,
):
    z, core = lax.axis_index("z"), lax.axis_index("core")
    even = core == 0
    olds = [
        pltpu.make_async_copy(source, old.at[k], sems.at[0, k])
        for k, source in enumerate((left_gram, right_gram, left_root, right_root))
    ]
    both = [
        pltpu.make_async_copy(source, powers.at[k], sems.at[1, k])
        for k, source in enumerate((squared, far_squared, root, far_root))
    ]
    load = pltpu.make_async_copy(stored, whole, sems.at[2, 0])
    for copy in [load] + olds + both:
        copy.start()
    load.wait()
    slab = whole[:, at(z * SIDE, SIDE, SIDE)]
    columns[...] = slab.astype(F32).T
    rows = whole[at((z * NC + core) * ROWS, ROWS, ROWS)]
    left = dot(rows, whole[...], ((1,), (1,)))
    turned = columns[at(core * ROWS, ROWS, ROWS)].astype(BF16)
    right = dot(turned, whole[...])
    for copy in olds + both[:2]:
        copy.wait()
    left = BETA * old[0] + left
    left_next[...] = left
    right = BETA * old[1] + right
    right_next[...] = right
    own, far = jnp.where(even, left, right), jnp.where(even, right, left)
    for _ in range(2):
        own, far = dot(own.astype(BF16), powers[0]), dot(far.astype(BF16), powers[1])
    for copy in both[2:]:
        copy.wait()
    own, far = dot(own.astype(BF16), powers[2]), dot(far.astype(BF16), powers[3])
    left_refined[...] = (5.0 * old[2] - jnp.where(even, own, far)) / 4.0
    right_refined[...] = (5.0 * old[3] - jnp.where(even, far, own)) / 4.0


def on_device(activations, cotangent, left_gram, right_gram, left_root, right_root):
    left_gram, right_gram = left_gram[0], right_gram[0]
    left_root, right_root = left_root[0], right_root[0]

    def pack(mate):
        return call(
            functools.partial(pack_kernel, mate),
            jax.ShapeDtypeStruct((TOKENS, ROOT + HALF), BF16), [HBM] * 4,
            scratch=[pltpu.VMEM((ROWS, BS), F32), pltpu.SemaphoreType.DMA((NX + 2,))],
            flops=100_000, moved=1_000_000,
        )(*map(in_hbm, (activations, cotangent, left_root, right_root)))

    far = pack(1)
    more = lax.ppermute(far, "core", SWAP)
    own = pack(0)
    more, own = lax.optimization_barrier((more, own))
    strip = call(
        strip_kernel, jax.ShapeDtypeStruct((TALL, STRIP), BF16), [VMEM, VMEM],
        scratch=[pltpu.VMEM((SIDE, BS), BF16)], moved=500_000,
    )(own, more)
    strip, more = lax.optimization_barrier((strip, more))
    strips = lax.all_gather(strip, "z", axis=0, tiled=True)
    partial = call(
        partial_kernel, jax.ShapeDtypeStruct((NZ, SLABS, WIDTH), BF16), [VMEM, VMEM],
        flops=2 * 256 * 2048 * 256, moved=3_000_000,
    )(own, more)
    parts = lax.all_to_all(partial, "z", 0, 0, tiled=True)
    copies = call(
        sum_kernel, jax.ShapeDtypeStruct((NX, NZ, ROWS, WIDTH), BF16), [VMEM],
        flops=1_000_000, moved=2_000_000,
    )(parts)
    root = call(
        root_kernel, jax.ShapeDtypeStruct((BS, BS), BF16), [VMEM], flops=1_000_000, moved=4_000_000
    )(strips)
    far_root = lax.ppermute(root, "core", SWAP)
    squared = call(
        square_kernel, jax.ShapeDtypeStruct((BS, BS), BF16), [VMEM], flops=2 * BS**3, moved=4_000_000
    )(root)
    far_squared = lax.ppermute(squared, "core", SWAP)
    mine = lax.all_to_all(
        copies.reshape(NX * NZ, ROWS, WIDTH), ("x", "z"), 0, 0, tiled=True
    ).reshape(NX, HALF, WIDTH)
    other = lax.ppermute(mine, "core", SWAP)

    first = call(
        first_kernel, jax.ShapeDtypeStruct((BS, BS), F32), [ANY] * 3,
        scratch=[
            pltpu.VMEM((HALF, BS), BF16),
            pltpu.VMEM((BS, HALF), BF16),
            pltpu.SemaphoreType.DMA((NX + 1,)),
        ],
        flops=BS**3, moved=3_000_000,
    )(mine, root, far_root)
    other, first = lax.optimization_barrier((other, first))
    square = pltpu.HBM((BS, BS), BF16)
    precond, whole = call(
        precond_kernel, (jax.ShapeDtypeStruct((NX, ROWS, WIDTH), BF16), square), [ANY] * 4 + [VMEM],
        places=(VMEM, HBM),
        scratch=[
            pltpu.VMEM((BS, BS), BF16),
            pltpu.VMEM((BS, HALF), BF16),
            pltpu.VMEM((BS, BS), BF16),
            pltpu.VMEM((TILE, BS), F32),
            pltpu.SemaphoreType.DMA((3, 4)),
        ],
        flops=4 * BS**3, moved=6_000_000,
    )(mine, other, root, far_root, first)
    arrived = lax.all_to_all(precond, "x", 0, 0, tiled=True)
    shape = jax.ShapeDtypeStruct((ROWS, BS), F32)
    outs = call(
        factor_kernel, (shape,) * 4, [HBM] * 5 + [ANY] * 4,
        scratch=[
            pltpu.VMEM((BS, BS), BF16),
            pltpu.VMEM((SIDE, BS), F32),
            pltpu.VMEM((4, ROWS, BS), F32),
            pltpu.VMEM((4, BS, BS), BF16),
            pltpu.SemaphoreType.DMA((3, 4)),
        ],
        flops=16 * 64 * 1024 * 1024, moved=8_000_000,
    )(*map(in_hbm, (whole, left_gram, right_gram, left_root, right_root)), squared, far_squared, root, far_root)
    return (*(o[None] for o in outs), arrived.astype(F32))


def solution(mesh):
    split = Mesh(mesh.devices.reshape(NZ, NC, NY, NX), (*TOK, *HID))
    factor = P(HID, TOK, None)
    return jax.shard_map(
        on_device,
        mesh=split,
        in_specs=(P(TOK, None), P(TOK, HID), factor, factor, factor, factor),
        out_specs=(factor, factor, factor, factor, P(None, TOK, HID)),
        check_vma=False,
    )
```

```python
import functools

import jax
import jax.numpy as jnp
from jax import lax
from jax.experimental import pallas as pl
from jax.experimental.pallas import tpu as pltpu
from jax.sharding import Mesh
from jax.sharding import PartitionSpec as P

BETA = 0.95
EPS = 1e-06
F32 = jnp.float32
BF16 = jnp.bfloat16
NZ, NC, NY, NX = 8, 2, 8, 4
BS = 1024
HALF = BS // NC
TOKENS = 128
ROWS = BS // (NZ * NC)
WIDTH = BS // NX
COT = NX * HALF
ROOT = COT + WIDTH
TILE = 512
SIDE = NC * ROWS
OFF = 3
SLABS = NX * ROWS
STRIP = (OFF + 1) * SIDE
EXTRA = ROWS * SIDE // STRIP
TALL = SIDE + EXTRA
TOK = ("z", "core")
HID = ("y", "x")
SWAP = [(0, 1), (1, 0)]
VMEM = pl.BlockSpec(memory_space=pltpu.VMEM)
ANY = pl.BlockSpec(memory_space=pl.ANY)
HBM = pl.BlockSpec(memory_space=pltpu.HBM)
PARAMS = pltpu.CompilerParams(vmem_limit_bytes=28 * 1024 * 1024)


def dot(a, b, dims=((1,), (0,))):
    return lax.dot_general(a, b, (dims, ((), ())), preferred_element_type=F32)


def call(body, outs, specs, scratch=(), flops=0, moved=0, places=None):
    return pl.pallas_call(
        body,
        out_shape=outs,
        in_specs=specs,
        out_specs=places or jax.tree.map(lambda _: VMEM, outs),
        scratch_shapes=list(scratch),
        compiler_params=PARAMS,
        cost_estimate=pl.CostEstimate(flops=flops, bytes_accessed=moved, transcendentals=0),
    )


def in_hbm(value):
    return pltpu.with_memory_space_constraint(value, pltpu.HBM)


def at(start, size, unit):
    return pl.ds(pl.multiple_of(start, unit), size)


def pack_kernel(mate, act, cot, left_root, right_root, out, root, sems):
    core = lax.axis_index("core")
    side = 1 - core if mate else core
    copies = [pltpu.make_async_copy(cot, out.at[:, pl.ds(COT, WIDTH)], sems.at[NX])]
    for r in range(NX):
        source = act.at[:, at(r * BS + side * HALF, HALF, 128)]
        copies.append(pltpu.make_async_copy(source, out.at[:, pl.ds(r * HALF, HALF)], sems.at[r]))
    for k, source in enumerate((left_root, right_root)):

        @pl.when(side == k)
        def _(source=source):
            pltpu.make_async_copy(source, root, sems.at[NX + 1]).start()

    for copy in copies:
        copy.start()
    pltpu.make_async_copy(left_root, root, sems.at[NX + 1]).wait()
    low = root[...].astype(BF16)
    out[:ROWS, ROOT:] = low[:, :HALF]
    out[ROWS:, ROOT:] = low[:, HALF:]
    for copy in copies:
        copy.wait()


def strip_kernel(own, more, strip, shard):
    z, core = lax.axis_index("z"), lax.axis_index("core")
    for given, side in ((own, core), (more, 1 - core)):
        rows = at(side * ROWS, ROWS, ROWS)
        shard[rows, :HALF] = given[:ROWS, ROOT:]
        shard[rows, HALF:] = given[ROWS:, ROOT:]
    def block(k):
        return shard[:, at(lax.rem(z + k, NZ) * SIDE, SIDE, SIDE)]

    for k in range(OFF + 1):
        strip[:SIDE, k * SIDE : (k + 1) * SIDE] = block(k)

    across = block(OFF + 1).astype(F32)
    half = jnp.where(z < NZ // 2, across.T[:ROWS], across[ROWS:]).astype(BF16)
    for k in range(OFF + 1):
        strip[SIDE:, k * SIDE : (k + 1) * SIDE] = half[k * EXTRA : (k + 1) * EXTRA]


def partial_kernel(own, more, out):
    for r in range(NX):
        cols = slice(r * HALF, (r + 1) * HALF)
        total = dot(own[:, cols], own[:, COT : COT + WIDTH], ((0,), (0,)))
        total += dot(more[:, cols], more[:, COT : COT + WIDTH], ((0,), (0,)))
        low = total.astype(BF16)
        for to in range(NZ):
            out[to, r * ROWS : (r + 1) * ROWS] = low[to * ROWS : (to + 1) * ROWS]


def sum_kernel(parts, out):
    for x in range(NX):
        rows = slice(x * ROWS, (x + 1) * ROWS)
        total = parts[0, rows].astype(F32)
        for z in range(1, NZ):
            total += parts[z, rows].astype(F32)
        low = total.astype(BF16)
        for z in range(NZ):
            out[x, z] = low


def root_kernel(strips, root):
    def cut(z):
        return slice(z * SIDE, (z + 1) * SIDE)

    for z in range(NZ):
        for k in range(OFF + 1):
            there = cut((z + k) % NZ)
            piece = strips[z * TALL : z * TALL + SIDE, k * SIDE : (k + 1) * SIDE]
            root[cut(z), there] = piece
            if k:
                root[there, cut(z)] = piece.T
    for z in range(NZ // 2):
        pieces = [
            strips[home * TALL + SIDE : (home + 1) * TALL, k * SIDE : (k + 1) * SIDE]
            for home in (z, z + NZ // 2)
            for k in range(OFF + 1)
        ]
        whole = jnp.concatenate(pieces, axis=0)
        root[cut(z + NZ // 2), cut(z)] = whole
        root[cut(z), cut(z + NZ // 2)] = whole.T


def first_kernel(mine, root, far_root, out, upper, left, sems):
    core = lax.axis_index("core")
    cols = at(core * HALF, HALF, 128)
    pieces = [
        pltpu.make_async_copy(mine.at[x], upper.at[:, pl.ds(x * WIDTH, WIDTH)], sems.at[x])
        for x in range(NX)
    ]
    for copy in pieces:
        copy.start()
    for side, source in enumerate((root, far_root)):

        @pl.when(core == side)
        def _(source=source):
            pltpu.make_async_copy(source.at[:, cols], left, sems.at[NX]).start()

    for copy in pieces + [pltpu.make_async_copy(root.at[:, cols], left, sems.at[NX])]:
        copy.wait()
    for i in range(0, BS, TILE):
        out[i : i + TILE] = dot(left[i : i + TILE], upper[...])


def precond_kernel(
    mine, other, root, far_root, first, out, stored, whole, left, right, kept, sems
):
    z, core = lax.axis_index("z"), lax.axis_index("core")
    place = (z * NC + core) * ROWS

    cols = at((1 - core) * HALF, HALF, 128)

    def bring(applied_by, second):
        return [
            pltpu.make_async_copy(applied_by.at[:, cols], left, sems.at[2, 0]),
            pltpu.make_async_copy(second, right, sems.at[2, 1]),
        ]

    pieces = []
    for k, (half, side) in enumerate(((mine, core), (other, 1 - core))):
        for x in range(NX):
            target = whole.at[at(side * HALF, HALF, HALF), pl.ds(x * WIDTH, WIDTH)]
            pieces.append(pltpu.make_async_copy(half.at[x], target, sems.at[k, x]))
    for copy in pieces:
        copy.start()

    @pl.when(core == 0)
    def _():
        for copy in bring(root, far_root):
            copy.start()

    @pl.when(core == 1)
    def _():
        for copy in bring(far_root, root):
            copy.start()

    applies, follows = bring(root, far_root)
    for copy in pieces + [applies]:
        copy.wait()
    store = pltpu.make_async_copy(whole, stored, sems.at[2, 2])
    store.start()

    total = jnp.zeros((1, BS), F32)
    for i in range(BS // TILE):
        part = slice(i * TILE, (i + 1) * TILE)
        lower = whole[at((1 - core) * HALF, HALF, HALF)]
        applied = (first[part] + dot(left[part], lower)).astype(BF16)
        if i == 0:
            follows.wait()
        precond = dot(applied, right[...])
        total += jnp.sum(precond * precond, axis=0, keepdims=True)

        @pl.when(i == place // TILE)
        def _(precond=precond):
            kept[...] = precond

    scale = 1.0 / jnp.sqrt(jnp.sum(total) / (BS * BS) + EPS)
    scaled = kept[at(place % TILE, ROWS, ROWS)] * scale
    for x in range(NX):
        out[x] = scaled[:, x * WIDTH : (x + 1) * WIDTH].astype(BF16)
    store.wait()


def square_kernel(root, squared):
    for i in range(0, BS, TILE):
        squared[i : i + TILE] = dot(root[i : i + TILE], root[...]).astype(BF16)


def factor_kernel(
    stored, left_gram, right_gram, left_root, right_root, squared, far_squared, root, far_root,
    left_next, right_next, left_refined, right_refined, whole, columns, old, powers, sems,
):
    z, core = lax.axis_index("z"), lax.axis_index("core")
    even = core == 0
    olds = [
        pltpu.make_async_copy(source, old.at[k], sems.at[0, k])
        for k, source in enumerate((left_gram, right_gram, left_root, right_root))
    ]
    both = [
        pltpu.make_async_copy(source, powers.at[k], sems.at[1, k])
        for k, source in enumerate((squared, far_squared, root, far_root))
    ]
    load = pltpu.make_async_copy(stored, whole, sems.at[2, 0])
    for copy in [load] + olds + both:
        copy.start()
    load.wait()
    slab = whole[:, at(z * SIDE, SIDE, SIDE)]
    columns[...] = slab.astype(F32).T
    rows = whole[at((z * NC + core) * ROWS, ROWS, ROWS)]
    left = dot(rows, whole[...], ((1,), (1,)))
    turned = columns[at(core * ROWS, ROWS, ROWS)].astype(BF16)
    right = dot(turned, whole[...])
    for copy in olds + both[:2]:
        copy.wait()
    left = BETA * old[0] + left
    left_next[...] = left
    right = BETA * old[1] + right
    right_next[...] = right
    own, far = jnp.where(even, left, right), jnp.where(even, right, left)
    for _ in range(2):
        own, far = dot(own.astype(BF16), powers[0]), dot(far.astype(BF16), powers[1])
    for copy in both[2:]:
        copy.wait()
    own, far = dot(own.astype(BF16), powers[2]), dot(far.astype(BF16), powers[3])
    left_refined[...] = (5.0 * old[2] - jnp.where(even, own, far)) / 4.0
    right_refined[...] = (5.0 * old[3] - jnp.where(even, far, own)) / 4.0


def on_device(activations, cotangent, left_gram, right_gram, left_root, right_root):
    left_gram, right_gram = left_gram[0], right_gram[0]
    left_root, right_root = left_root[0], right_root[0]

    def pack(mate):
        return call(
            functools.partial(pack_kernel, mate),
            jax.ShapeDtypeStruct((TOKENS, ROOT + HALF), BF16), [HBM] * 4,
            scratch=[pltpu.VMEM((ROWS, BS), F32), pltpu.SemaphoreType.DMA((NX + 2,))],
            flops=100_000, moved=1_000_000,
        )(*map(in_hbm, (activations, cotangent, left_root, right_root)))

    far = pack(1)
    more = lax.ppermute(far, "core", SWAP)
    own = pack(0)
    more, own = lax.optimization_barrier((more, own))
    partial = call(
        partial_kernel, jax.ShapeDtypeStruct((NZ, SLABS, WIDTH), BF16), [VMEM, VMEM],
        flops=2 * 256 * 2048 * 256, moved=3_000_000,
    )(own, more)
    partial, more = lax.optimization_barrier((partial, more))
    strip = call(
        strip_kernel, jax.ShapeDtypeStruct((TALL, STRIP), BF16), [VMEM, VMEM],
        scratch=[pltpu.VMEM((SIDE, BS), BF16)], moved=500_000,
    )(own, more)
    strips = lax.all_gather(strip, "z", axis=0, tiled=True)
    parts = lax.all_to_all(partial, "z", 0, 0, tiled=True)
    copies = call(
        sum_kernel, jax.ShapeDtypeStruct((NX, NZ, ROWS, WIDTH), BF16), [VMEM],
        flops=1_000_000, moved=2_000_000,
    )(parts)
    root = call(
        root_kernel, jax.ShapeDtypeStruct((BS, BS), BF16), [VMEM], flops=1_000_000, moved=4_000_000
    )(strips)
    far_root = lax.ppermute(root, "core", SWAP)
    squared = call(
        square_kernel, jax.ShapeDtypeStruct((BS, BS), BF16), [VMEM], flops=2 * BS**3, moved=4_000_000
    )(root)
    far_squared = lax.ppermute(squared, "core", SWAP)
    mine = lax.all_to_all(
        copies.reshape(NX * NZ, ROWS, WIDTH), ("x", "z"), 0, 0, tiled=True
    ).reshape(NX, HALF, WIDTH)
    other = lax.ppermute(mine, "core", SWAP)

    first = call(
        first_kernel, jax.ShapeDtypeStruct((BS, BS), F32), [ANY] * 3,
        scratch=[
            pltpu.VMEM((HALF, BS), BF16),
            pltpu.VMEM((BS, HALF), BF16),
            pltpu.SemaphoreType.DMA((NX + 1,)),
        ],
        flops=BS**3, moved=3_000_000,
    )(mine, root, far_root)
    other, first = lax.optimization_barrier((other, first))
    square = pltpu.HBM((BS, BS), BF16)
    precond, whole = call(
        precond_kernel, (jax.ShapeDtypeStruct((NX, ROWS, WIDTH), BF16), square), [ANY] * 4 + [VMEM],
        places=(VMEM, HBM),
        scratch=[
            pltpu.VMEM((BS, BS), BF16),
            pltpu.VMEM((BS, HALF), BF16),
            pltpu.VMEM((BS, BS), BF16),
            pltpu.VMEM((TILE, BS), F32),
            pltpu.SemaphoreType.DMA((3, 4)),
        ],
        flops=4 * BS**3, moved=6_000_000,
    )(mine, other, root, far_root, first)
    arrived = lax.all_to_all(precond, "x", 0, 0, tiled=True)
    shape = jax.ShapeDtypeStruct((ROWS, BS), F32)
    outs = call(
        factor_kernel, (shape,) * 4, [HBM] * 5 + [ANY] * 4,
        scratch=[
            pltpu.VMEM((BS, BS), BF16),
            pltpu.VMEM((SIDE, BS), F32),
            pltpu.VMEM((4, ROWS, BS), F32),
            pltpu.VMEM((4, BS, BS), BF16),
            pltpu.SemaphoreType.DMA((3, 4)),
        ],
        flops=16 * 64 * 1024 * 1024, moved=8_000_000,
    )(*map(in_hbm, (whole, left_gram, right_gram, left_root, right_root)), squared, far_squared, root, far_root)
    return (*(o[None] for o in outs), arrived.astype(F32))


def solution(mesh):
    split = Mesh(mesh.devices.reshape(NZ, NC, NY, NX), (*TOK, *HID))
    factor = P(HID, TOK, None)
    return jax.shard_map(
        on_device,
        mesh=split,
        in_specs=(P(TOK, None), P(TOK, HID), factor, factor, factor, factor),
        out_specs=(factor, factor, factor, factor, P(None, TOK, HID)),
        check_vma=False,
    )
```
